32 devices in a mesh: crop: 2 (over core), pix: 16 (over z, y, x).
Axes of the slice: x: 2, y: 2, z: 4, core: 2. Of those that a mesh axis runs over, the one named last changes fastest.
Arguments:
- inputs: bfloat16 [2, 256, 64, 2016], P('crop', 'pix'), may hold values from -6 to 6
- out_grad: bfloat16 [2, 256, 64, 2016], P('crop', 'pix'), may hold values from -6 to 6
- pixel_mask: int32 [2, 256, 64], P('crop', 'pix'), may hold values from 0 to 1, as said below
- crop_source: int32 [256], P('pix'), may hold values from 0 to 255
- packed: float32 [4032, 2772], P('pix')
- moment_one: float32 [4032, 2772], P('pix'), may hold values from -0.00048828125 to 0.00048828125
- moment_two: float32 [4032, 2772], P('pix'), may hold values from 8.935496e-11 to 3.5741984e-10
- vector: float32 [14616], replicated
- vector_one: float32 [14616], replicated, may hold values from -0.00048828125 to 0.00048828125
- vector_two: float32 [14616], replicated, may hold values from 8.935496e-11 to 3.5741984e-10
Outputs:
- output: bfloat16 [2, 256, 64, 2016], P('crop', 'pix')
- input_grad: float32 [2, 256, 64, 2016], P('crop', 'pix')
- packed_new: float32 [4032, 2772], P('pix')
- moment_one_new: float32 [4032, 2772], P('pix')
- moment_two_new: float32 [4032, 2772], P('pix')
- vector_new: float32 [14616], replicated
- vector_one_new: float32 [14616], replicated
- vector_two_new: float32 [14616], replicated
- grad_norm: float32 [], replicated
The draws below stay inside these ranges and needn't reach their ends.
Inputs may be any that keep to these rules, and one draw needn't show every extreme that they name: `pixel_mask`: each image's valid pixels form a rectangle of 2 to 8 rows by 2 to 8 columns at the top left of its 8 x 8 grid.
All inputs are finite; a program needn't handle non-finite values.
Results may differ from the reference program's by a relative error of at most 0.013.
The reference program's roundings to bfloat16 on the way count: a program that leaves them out, or rounds other values in their place, can miss the bound.
Values may be sent and summed in bfloat16 or wider, within the bound.
No kernel may reach another device: no remote copies, remote signals or barrier semaphores. Data moves between devices by JAX's collectives and lax.ppermute only.
A program may use at most 448 MiB of HBM per device.

```python
import math
import jax
import jax.numpy as jnp
from jax import lax

W = 2016
GW = 56
R = 504
GRID = 8
IMG_DEV = 16
STEP = 10
IMAGES = 256
PC = 2772
VEC = 14616
NPARAM = 11191320


def draw_pixel_mask(key, part):
    key = jax.random.fold_in(key, 3)
    subkeys = jax.random.split(key, 2)
    crop_index = jnp.arange(2, dtype=jnp.int32)[:, None]
    images = jnp.arange(IMAGES, dtype=jnp.int32)[None, :]
    devices = IMAGES // IMG_DEV
    device = images // IMG_DEV
    base_side = 2 + 6 * device // jnp.maximum(devices - 1, 1)
    height = jnp.clip(base_side - crop_index + jax.random.randint(subkeys[0], (2, IMAGES), -1, 2), 2, GRID)
    breadth = jnp.clip(base_side - crop_index + jax.random.randint(subkeys[1], (2, IMAGES), -1, 2), 2, GRID)
    cell_index = jnp.arange(GRID * GRID, dtype=jnp.int32)
    inside = ((cell_index // GRID)[None, None, :] < height[:, :, None]) & ((cell_index % GRID)[None, None, :] < breadth[:, :, None])
    return inside.astype(jnp.int32)


def draw_packed(key, part):
    key = jax.random.fold_in(key, 5)
    scales = jnp.concatenate([jnp.full((W,), W ** (-0.5), jnp.float32), jnp.full((9 * GW // 2,), (9 * GW) ** (-0.5), jnp.float32), jnp.full((R // 2,), W ** (-0.5), jnp.float32), jnp.full((R // 2,), R ** (-0.5), jnp.float32)])
    values = jax.random.normal(key, (2 * W, PC), jnp.float32)
    return values * scales[None, :]


def draw_vector(key, part):
    key = jax.random.fold_in(key, 7)
    subkeys = jax.random.split(key, 2)
    position = jnp.arange(W, dtype=jnp.float32) / (W - 1)
    rising = 1.0 + 2.0 * position
    jitter = jnp.exp(jax.random.uniform(subkeys[0], (3, W), jnp.float32, -0.2, 0.2))
    shifts = 0.35 * jax.random.normal(subkeys[1], (4 * W + R,), jnp.float32)
    return jnp.concatenate([(rising[None, :] * jitter).reshape(3 * W), shifts])


def with_ends(array, rng, low, high):
    spot = [jax.random.randint(jax.random.fold_in(rng, axis), (), 0, length) for axis, length in enumerate(array.shape)]
    widest = array.shape.index(max(array.shape))
    next_to = spot[:widest] + [(spot[widest] + 1) % array.shape[widest]] + spot[widest + 1:]
    return array.at[tuple(spot)].set(low).at[tuple(next_to)].set(high)


def shard_levels(own_key, extent, cuts, least, top_value):
    def one(dim, shards_of):
        steps = jax.random.uniform(jax.random.fold_in(jax.random.fold_in(own_key, 6), dim), (shards_of,), jnp.float32, least / len(cuts), top_value / len(cuts))
        return jnp.repeat(jnp.exp(steps), extent[dim] // shards_of).reshape((-1,) + (1,) * (len(extent) - dim - 1))

    level = one(*cuts[0])
    for cut in cuts[1:]:
        level = level * one(*cut)
    return level


def normal_values(own_key, extent, width, limit, pieces=(), kind=jnp.bfloat16):
    values = jax.random.normal(own_key, extent, jnp.float32) * width
    if len(pieces) > 0:
        values = shard_levels(own_key, extent, pieces, -0.22, 0.18) * values
    return jnp.clip(values, min=-limit, max=limit).astype(kind)


def setup_inputs(seed: int = 0) -> dict:
    key_list = jax.random.split(jax.random.key(seed), 11)
    return {
        "inputs": normal_values(key_list[0], (2, IMAGES, GRID * GRID, W), 1.0, 6.0, ((0, 2), (1, 16))),
        "out_grad": normal_values(key_list[1], (2, IMAGES, GRID * GRID, W), 1.0, 6.0, ((0, 2), (1, 16))),
        "pixel_mask": draw_pixel_mask(jax.random.fold_in(key_list[10], 71), 0),
        "crop_source": with_ends(jax.random.randint(key_list[3], (IMAGES,), 0, IMAGES), jax.random.fold_in(key_list[3], 1), 0, IMAGES - 1).astype(jnp.int32),
        "packed": draw_packed(jax.random.fold_in(key_list[10], 71), 0),
        "moment_one": normal_values(key_list[5], (2 * W, PC), (0.11 / NPARAM ** 0.5), 0.00048828125, ((0, 16),), jnp.float32),
        "moment_two": jnp.clip(jnp.exp(math.log(3.574198437217291e-10) - 1.3862944 * jax.random.uniform(key_list[6], (2 * W, PC), jnp.float32) ** shard_levels(key_list[6], (2 * W, PC), ((0, 16),), -0.2, 0.2)), 8.935496093043227e-11, 3.574198437217291e-10),
        "vector": draw_vector(jax.random.fold_in(key_list[10], 71), 0),
        "vector_one": normal_values(key_list[8], (VEC,), (0.11 / NPARAM ** 0.5), 0.00048828125, (), jnp.float32),
        "vector_two": jnp.clip(jnp.exp(jax.random.uniform(key_list[9], (VEC,), jnp.float32, math.log(8.935496093043227e-11), math.log(3.574198437217291e-10))), 8.935496093043227e-11, 3.574198437217291e-10),
    }


@jax.custom_vjp
def low(v):
    return lax.optimization_barrier(v.astype(jnp.bfloat16)).astype(jnp.float32)

@jax.custom_vjp
def low_back(v):
    return v

def low_keep(v):
    return (low(v), None)

def low_pass(kept, grad):
    return (grad,)

def back_keep(v):
    return (v, None)

def back_low(kept, grad):
    return (low(grad),)
low.defvjp(low_keep, low_pass)
low_back.defvjp(back_keep, back_low)
highest = lax.Precision.HIGHEST
epsilon_norm = 1e-05
align_weight = 16.0
clip_bound = 1.0
beta_one = 0.9
beta_two = 0.999
adam_epsilon = 1e-08
rate_matrix = 0.02
rate_vector = 0.4
decay_matrix = 0.05

def unpack(packed):
    half_width = W // 2
    kernel_end = W + 9 * GW // 2
    first_weight = packed[:, :half_width].reshape(W, W)
    third_weight = packed[:, half_width:W].reshape(W, W)
    conv_weight = packed[:, W:kernel_end].reshape(W // GW, 9, GW, GW)
    squeeze_weight = packed[:, kernel_end:kernel_end + R // 2].reshape(W, R)
    excite_weight = packed[:, kernel_end + R // 2:].reshape(W, R)
    return (first_weight, third_weight, conv_weight, squeeze_weight, excite_weight)

def split_vector(vector):
    norm_gains = vector[:3 * W].reshape(3, W)
    shifts = vector[3 * W:6 * W].reshape(3, W)
    return (norm_gains, shifts, vector[6 * W:7 * W], vector[7 * W:])

def contract_last(left, right):
    return lax.dot_general(left, right, (((1,), (1,)), ((), ())), precision=highest)

def masked_norm(values, valid_rows, valid_count, norm_gain, shift):
    channel_mean = lax.optimization_barrier(jnp.sum(values * valid_rows, axis=0)) / valid_count
    centered = values - channel_mean
    spread = lax.optimization_barrier(jnp.sum(centered * centered * valid_rows, axis=0)) / valid_count
    return norm_gain * (centered * lax.rsqrt(spread + epsilon_norm)) + shift

def grouped_conv(hidden, conv_weight):
    images = hidden.shape[0] // (GRID * GRID)
    image_grid = hidden.reshape(images, GRID, GRID, W // GW, GW)
    padded = jnp.pad(image_grid, ((0, 0), (1, 1), (1, 1), (0, 0), (0, 0)))
    summed_taps = jnp.zeros(image_grid.shape, jnp.float32)
    for offset in range(9):
        row_start = offset // 3
        col_start = offset % 3
        window_cells = padded[:, row_start:row_start + GRID, col_start:col_start + GRID]
        summed_taps = summed_taps + jnp.einsum('nyxgi,gio->nyxgo', window_cells, conv_weight[:, offset], precision=highest)
    return summed_taps.reshape(images * GRID * GRID, W)

def forward(inputs, packed, vector, pixel_mask, crop_source):
    first_weight, third_weight, conv_weight, squeeze_weight, excite_weight = unpack(low(packed))
    norm_gains, shifts, excite_bias, squeeze_bias = split_vector(vector)
    images = 2 * IMAGES
    pixel_rows = inputs.reshape(images * GRID * GRID, W)
    valid_rows = pixel_mask.reshape(images * GRID * GRID, 1).astype(jnp.float32)
    valid_count = jnp.sum(valid_rows)
    per_image = lax.optimization_barrier(jnp.sum(pixel_mask.reshape(images, GRID * GRID).astype(jnp.float32), axis=1))[:, None]
    first_out = low_back(contract_last(pixel_rows, first_weight))
    hidden_one = low(jax.nn.silu(masked_norm(first_out, valid_rows, valid_count, norm_gains[0], shifts[0])) * valid_rows)
    conv_out = low_back(grouped_conv(hidden_one, conv_weight))
    hidden_two = jax.nn.silu(masked_norm(conv_out, valid_rows, valid_count, norm_gains[1], shifts[1])) * valid_rows
    pooled = low(lax.optimization_barrier(jnp.sum(hidden_two.reshape(images, GRID * GRID, W), axis=1)) / per_image)
    squeeze_pre = low_back(jnp.dot(pooled, squeeze_weight, precision=highest) + squeeze_bias)
    squeezed = low(jax.nn.silu(squeeze_pre))
    excite_pre = low_back(contract_last(squeezed, excite_weight) + excite_bias)
    excite_gate = jax.nn.sigmoid(excite_pre)
    scaled = low((hidden_two.reshape(images, GRID * GRID, W) * excite_gate[:, None, :]).reshape(images * GRID * GRID, W))
    third_out = low_back(contract_last(scaled, third_weight))
    output = jax.nn.silu(masked_norm(third_out, valid_rows, valid_count, norm_gains[2], shifts[2]) + pixel_rows) * valid_rows
    embedded = lax.optimization_barrier(jnp.sum(output.reshape(images, GRID * GRID, W), axis=1)) / per_image
    global_embed = low(embedded[:IMAGES])
    source_hits = (crop_source[:, None] == jnp.arange(IMAGES, dtype=jnp.int32)[None, :]).astype(jnp.float32)
    crop_counts = lax.optimization_barrier(jnp.sum(source_hits, axis=0))
    matched = jnp.dot(source_hits, global_embed, precision=highest)
    divisor = jnp.dot(source_hits, crop_counts, precision=highest)
    aligned = align_weight * jnp.sum(lax.optimization_barrier(jnp.sum(embedded[IMAGES:] * matched, axis=1)) / divisor)
    return (output.reshape(2, IMAGES, GRID * GRID, W), aligned)

def adam_step(parameter, gradient, first_moment, second_moment, step_rate, decay_rate):
    first_new = beta_one * first_moment + (1.0 - beta_one) * gradient
    second_new = beta_two * second_moment + (1.0 - beta_two) * gradient * gradient
    corrected = first_new / (1.0 - beta_one ** STEP) / (jnp.sqrt(second_new / (1.0 - beta_two ** STEP)) + adam_epsilon)
    return (parameter - step_rate * (corrected + decay_rate * parameter), first_new, second_new)

def reference(inputs, out_grad, pixel_mask, crop_source, packed, moment_one, moment_two, vector, vector_one, vector_two):

    def wrapped(inputs_wide, packed_wide, vector_wide):
        return forward(inputs_wide, packed_wide, vector_wide, pixel_mask, crop_source)
    (output, aligned), pullback = jax.vjp(wrapped, inputs.astype(jnp.float32), packed, vector)
    input_grad, packed_grad, vector_grad = pullback((out_grad.astype(jnp.float32), jnp.ones((), jnp.float32)))
    grad_norm = jnp.sqrt(jnp.sum(packed_grad * packed_grad) + jnp.sum(vector_grad * vector_grad))
    factor = jnp.minimum(1.0, clip_bound / (grad_norm + 1e-06))
    packed_new, moment_one_new, moment_two_new = adam_step(packed, factor * packed_grad, moment_one, moment_two, rate_matrix, decay_matrix)
    vector_new, vector_first, vector_second = adam_step(vector, factor * vector_grad, vector_one, vector_two, rate_vector, 0.0)
    return (output.astype(jnp.bfloat16), input_grad, packed_new, moment_one_new, moment_two_new, vector_new, vector_first, vector_second, grad_norm)
```

```python
import jax
import jax.numpy as jnp
from jax import lax
from jax.experimental import pallas as pl
from jax.experimental.pallas import tpu as pltpu
from jax.sharding import PartitionSpec as P

W = 2016
GW = 56
R = 504
GRID = 8
PIX = GRID * GRID
STEP = 10
SB = 224
SP = 256
NB = W // SB
WP = NB * SP
RP = 512

epsilon_norm = 1e-05
align_weight = 16.0
clip_bound = 1.0
beta_one = 0.9
beta_two = 0.999
adam_epsilon = 1e-08
rate_matrix = 0.02
rate_vector = 0.4
decay_matrix = 0.05

f32 = jnp.float32
bf16 = jnp.bfloat16
MiB = 1024 * 1024


def params(mib):
    return pltpu.CompilerParams(vmem_limit_bytes=mib * MiB)


def cost(flops, nbytes, exps=0):
    return pl.CostEstimate(flops=flops, bytes_accessed=nbytes, transcendentals=exps)


def nn(a, b):
    return lax.dot_general(a, b, (((1,), (0,)), ((), ())), preferred_element_type=f32)


def nt(a, b):
    return lax.dot_general(a, b, (((1,), (1,)), ((), ())), preferred_element_type=f32)


def tn(a, b):
    return lax.dot_general(a, b, (((0,), (0,)), ((), ())), preferred_element_type=f32)


def sigmoid(t):
    return 0.5 * jnp.tanh(0.5 * t) + 0.5


def over_pixels(per_image, rows):
    images, width = per_image.shape
    wide = jnp.broadcast_to(per_image[:, None, :], (images, PIX, width))
    return wide.reshape(rows, width)


def image_sum(values):
    rows, width = values.shape
    return jnp.sum(values.reshape(rows // PIX, PIX, width), axis=1)


def local_moments(a, v):
    count = jnp.sum(v)
    mean = jnp.sum(a * v, axis=0, keepdims=True) / count
    centered = a - mean
    return mean, jnp.sum(centered * centered * v, axis=0, keepdims=True)


def first_kernel(x_ref, f_ref, v_ref, a_ref, st_ref):
    a = nt(x_ref[...], f_ref[...])
    mean, squares = local_moments(a, v_ref[...])
    a_ref[...] = jnp.zeros_like(a_ref)
    st_ref[...] = jnp.zeros_like(st_ref)
    a_ref[:, :SB] = a
    st_ref[0:1, :SB] = mean
    st_ref[1:2, :SB] = squares


def first_matmul(x, f, v):
    rows = x.shape[0]
    return pl.pallas_call(
        first_kernel,
        grid=(NB,),
        in_specs=[
            pl.BlockSpec((rows, W), lambda j: (0, 0)),
            pl.BlockSpec((SB, W), lambda j: (j, 0)),
            pl.BlockSpec((rows, 1), lambda j: (0, 0)),
        ],
        out_specs=[
            pl.BlockSpec((rows, SP), lambda j: (0, j)),
            pl.BlockSpec((2, SP), lambda j: (0, j)),
        ],
        out_shape=[
            jax.ShapeDtypeStruct((rows, WP), f32),
            jax.ShapeDtypeStruct((2, WP), f32),
        ],
        compiler_params=params(40),
        cost_estimate=cost(2 * rows * W * WP, 24 * MiB),
        name="first_matmul",
    )(x, f, v)


def shifted(values, row_step, col_step, sub):
    rows, width = values.shape
    if col_step == -1:
        values = jnp.where(sub == 0, 0.0, pltpu.roll(values, 1, 0))
    elif col_step == 1:
        values = jnp.where(sub == GRID - 1, 0.0, pltpu.roll(values, rows - 1, 0))
    if row_step:
        grid = values.reshape(rows // PIX, PIX, width)
        edge = jnp.zeros((rows // PIX, GRID, width), values.dtype)
        if row_step == -1:
            grid = jnp.concatenate([edge, grid[:, : PIX - GRID]], axis=1)
        else:
            grid = jnp.concatenate([grid[:, GRID:], edge], axis=1)
        values = grid.reshape(rows, width)
    return values


def spread_taps(values, scratch, sign):
    sub = lax.broadcasted_iota(jnp.int32, values.shape, 0) & (GRID - 1)
    for dx in range(3):
        moved = shifted(values, 0, sign * (dx - 1), sub)
        for dy in range(3):
            tap = 3 * dy + dx
            scratch[:, tap * SP : (tap + 1) * SP] = shifted(
                moved, sign * (dy - 1), 0, sub
            ).astype(bf16)


def group_of(shape, axis):
    at = lax.broadcasted_iota(jnp.int32, shape, axis)
    return (
        (at >= GW).astype(jnp.int32)
        + (at >= 2 * GW).astype(jnp.int32)
        + (at >= 3 * GW).astype(jnp.int32)
        + (at >= 4 * GW).astype(jnp.int32)
    )


def lane_copies():
    out = lax.broadcasted_iota(jnp.int32, (GW, SP), 0)
    lane = lax.broadcasted_iota(jnp.int32, (GW, SP), 1)
    within = lane - GW * group_of((GW, SP), 1)
    return ((within == out) & (lane < SB)).astype(f32).astype(bf16)


def block_mask():
    return group_of((SB, SP), 0) == group_of((SB, SP), 1)


def build_blocks(k_ref, w_scr):
    copies = lane_copies()
    mask = block_mask()
    for tap in range(9):
        stack = jnp.concatenate([k_ref[q, tap].astype(f32) for q in range(4)], axis=0)
        wide = nn(stack.astype(bf16), copies)
        w_scr[tap * SP : tap * SP + SB, :] = jnp.where(mask, wide, 0.0).astype(bf16)
        w_scr[tap * SP + SB : (tap + 1) * SP, :] = jnp.zeros((SP - SB, SP), bf16)


def conv_kernel(a_ref, p_ref, v_ref, k_ref, c_ref, st_ref, taps, w_scr):
    v = v_ref[...]
    b = (a_ref[...] - p_ref[0:1, :]) * p_ref[1:2, :] + p_ref[2:3, :]
    h = b * sigmoid(b) * v
    spread_taps(h, taps, 1)
    build_blocks(k_ref, w_scr)
    c = nn(taps[...], w_scr[...])
    c_ref[...] = c
    mean, squares = local_moments(c, v)
    st_ref[0:1, :] = mean
    st_ref[1:2, :] = squares


def conv_forward(a, p, v, k):
    rows = a.shape[0]
    return pl.pallas_call(
        conv_kernel,
        grid=(NB,),
        in_specs=[
            pl.BlockSpec((rows, SP), lambda j: (0, j)),
            pl.BlockSpec((8, SP), lambda j: (0, j)),
            pl.BlockSpec((rows, 1), lambda j: (0, 0)),
            pl.BlockSpec((4, 9, GW, GW), lambda j: (j, 0, 0, 0)),
        ],
        out_specs=[
            pl.BlockSpec((rows, SP), lambda j: (0, j)),
            pl.BlockSpec((2, SP), lambda j: (0, j)),
        ],
        out_shape=[
            jax.ShapeDtypeStruct((rows, WP), f32),
            jax.ShapeDtypeStruct((2, WP), f32),
        ],
        scratch_shapes=[pltpu.VMEM((rows, 9 * SP), bf16), pltpu.VMEM((9 * SP, SP), bf16)],
        compiler_params=params(40),
        cost_estimate=cost(2 * rows * 9 * SP * WP, 24 * MiB),
        name="conv_forward",
    )(a, p, v, k)


def third_kernel(
    c_ref, p_ref, v_ref, ninv_ref, qe_ref, eb_ref, qb_ref, l_ref,
    a3_ref, st_ref, sp_ref, zp_ref, z_ref, gate_ref,
    h2_scr, e_scr, u_scr,
):
    step = pl.program_id(0)
    rows = v_ref.shape[0]

    @pl.when(step == 0)
    def _():
        zp_ref[...] = jnp.broadcast_to(qb_ref[...], zp_ref.shape)

    @pl.when(step < NB)
    def _():
        b = (c_ref[...] - p_ref[0:1, :]) * p_ref[1:2, :] + p_ref[2:3, :]
        h = b * sigmoid(b) * v_ref[...]
        h2_scr[step] = h
        pooled = (image_sum(h) * ninv_ref[...]).astype(bf16)
        sp_ref[step] = pooled
        zp_ref[...] += nn(pooled[:, :SB], qe_ref[:, :RP])
        e_scr[step] = qe_ref[:, RP:]

    @pl.when(step == NB)
    def _():
        zp = zp_ref[...]
        z = (zp * sigmoid(zp)).astype(bf16)
        z_ref[...] = z
        gate_ref[...] = jnp.zeros_like(gate_ref)
        for j in range(NB):
            gate_ref[j, :, :SB] = sigmoid(nt(z, e_scr[j]) + eb_ref[j, :, :SB])
            u = h2_scr[j] * over_pixels(gate_ref[j], rows)
            u_scr[:, j * SP : (j + 1) * SP] = u.astype(bf16)

    @pl.when(step >= NB)
    def _():
        a3 = nt(u_scr[...], l_ref[...])
        a3_ref[...] = a3
        mean, squares = local_moments(a3, v_ref[...])
        st_ref[0:1, :] = mean
        st_ref[1:2, :] = squares


def third_matmul(c, p, v, ninv, qe, eb, qb, l):
    rows = c.shape[0]
    images = rows // PIX
    first = lambda i: jnp.minimum(i, NB - 1)
    then = lambda i: jnp.maximum(i - NB, 0)
    blocks = pl.cdiv(W, SP)
    return pl.pallas_call(
        third_kernel,
        grid=(NB + blocks,),
        in_specs=[
            pl.BlockSpec((rows, SP), lambda i: (0, first(i))),
            pl.BlockSpec((8, SP), lambda i: (0, first(i))),
            pl.BlockSpec((rows, 1), lambda i: (0, 0)),
            pl.BlockSpec((images, 1), lambda i: (0, 0)),
            pl.BlockSpec((SB, 2 * RP), lambda i: (first(i), 0)),
            pl.BlockSpec((NB, 1, SP), lambda i: (0, 0, 0)),
            pl.BlockSpec((1, RP), lambda i: (0, 0)),
            pl.BlockSpec((SP, WP), lambda i: (then(i), 0)),
        ],
        out_specs=[
            pl.BlockSpec((rows, SP), lambda i: (0, then(i))),
            pl.BlockSpec((2, SP), lambda i: (0, then(i))),
            pl.BlockSpec((NB, images, SP), lambda i: (0, 0, 0)),
            pl.BlockSpec((images, RP), lambda i: (0, 0)),
            pl.BlockSpec((images, RP), lambda i: (0, 0)),
            pl.BlockSpec((NB, images, SP), lambda i: (0, 0, 0)),
        ],
        out_shape=[
            jax.ShapeDtypeStruct((rows, W), f32),
            jax.ShapeDtypeStruct((2, W), f32),
            jax.ShapeDtypeStruct((NB, images, SP), bf16),
            jax.ShapeDtypeStruct((images, RP), f32),
            jax.ShapeDtypeStruct((images, RP), bf16),
            jax.ShapeDtypeStruct((NB, images, SP), f32),
        ],
        scratch_shapes=[
            pltpu.VMEM((NB, rows, SP), f32),
            pltpu.VMEM((NB, SB, RP), bf16),
            pltpu.VMEM((rows, WP), bf16),
        ],
        compiler_params=params(50),
        cost_estimate=cost(2 * rows * W * WP, 32 * MiB),
        name="third_matmul",
    )(c, p, v, ninv, qe, eb, qb, l)


IMGS = 4


def output_kernel(a3_ref, x_ref, og_ref, p_ref, v_ref, ninv_ref, out_ref, im_ref, t_ref):
    step = pl.program_id(0)
    v = v_ref[...]
    normed = (a3_ref[...] - p_ref[0:1, :]) * p_ref[1:2, :]
    total = p_ref[2:3, :] * normed + p_ref[3:4, :] + x_ref[...].astype(f32)
    logistic = sigmoid(total)
    out = total * logistic * v
    out_ref[...] = out.astype(bf16)
    slope = logistic * (1.0 + total * (1.0 - logistic)) * v
    im_ref[0, 0] = image_sum(out) * ninv_ref[0]
    im_ref[0, 1] = image_sum(slope)
    slope_normed = slope * normed
    im_ref[0, 2] = image_sum(slope_normed)
    og = og_ref[...].astype(f32)
    one = jnp.sum(og * slope_normed, axis=0, keepdims=True)
    two = jnp.sum(og * slope, axis=0, keepdims=True)

    @pl.when(step == 0)
    def _():
        t_ref[...] = jnp.zeros_like(t_ref)

    t_ref[0:1, :] += one
    t_ref[1:2, :] += two


def output_pass(a3, x, og, p, v, ninv):
    rows = x.shape[0]
    images = rows // PIX
    steps = images // IMGS
    part = IMGS * PIX
    return pl.pallas_call(
        output_kernel,
        grid=(steps,),
        in_specs=[
            pl.BlockSpec((part, W), lambda i: (i, 0)),
            pl.BlockSpec((part, W), lambda i: (i, 0)),
            pl.BlockSpec((part, W), lambda i: (i, 0)),
            pl.BlockSpec((8, W), lambda i: (0, 0)),
            pl.BlockSpec((part, 1), lambda i: (i, 0)),
            pl.BlockSpec((1, IMGS, 1), lambda i: (i, 0, 0)),
        ],
        out_specs=[
            pl.BlockSpec((part, W), lambda i: (i, 0)),
            pl.BlockSpec((1, 3, IMGS, W), lambda i: (i, 0, 0, 0)),
            pl.BlockSpec((2, W), lambda i: (0, 0)),
        ],
        out_shape=[
            jax.ShapeDtypeStruct((rows, W), bf16),
            jax.ShapeDtypeStruct((steps, 3, IMGS, W), f32),
            jax.ShapeDtypeStruct((2, W), f32),
        ],
        compiler_params=params(40),
        cost_estimate=cost(30 * rows * W, 24 * MiB, 2 * rows * W),
        name="output_pass",
    )(a3, x, og, p, v, ninv.reshape(steps, IMGS, 1))


def third_back_kernel(
    a3_ref, x_ref, og_ref, p_ref, v_ref, den_ref, l_ref, c_ref, p2_ref, vall_ref, gate_ref,
    dv_ref, gl_ref, du_ref, im_ref,
    da_scr, dat_scr,
):
    step = pl.program_id(0)
    rows = vall_ref.shape[0]
    part = v_ref.shape[0]
    steps = rows // part

    @pl.when(step < steps)
    def _():
        v = v_ref[...]
        normed = (a3_ref[...] - p_ref[0:1, :]) * p_ref[1:2, :]
        total = p_ref[2:3, :] * normed + p_ref[3:4, :] + x_ref[...].astype(f32)
        logistic = sigmoid(total)
        slope = logistic * (1.0 + total * (1.0 - logistic)) * v
        dv = (og_ref[...].astype(f32) + over_pixels(den_ref[0], part)) * slope
        dv_ref[...] = dv
        da = v * p_ref[4:5, :] * (dv - (p_ref[5:6, :] + normed * p_ref[6:7, :]))
        low = da.astype(bf16)
        da_scr[pl.ds(pl.multiple_of(step * part, part), part), :] = low
        dat_scr[:, pl.ds(pl.multiple_of(step * part, part), part)] = da.T.astype(bf16)

    @pl.when(step >= steps)
    def _():
        v = vall_ref[...]
        du = nn(da_scr[...], l_ref[...])
        du_ref[...] = du
        normed = (c_ref[...] - p2_ref[0:1, :]) * p2_ref[1:2, :]
        b = p2_ref[2:3, :] * normed + p2_ref[3:4, :]
        logistic = sigmoid(b)
        h = b * logistic * v
        u = (h * over_pixels(gate_ref[0], rows)).astype(bf16)
        gl_ref[...] = nn(dat_scr[...], u).astype(bf16)
        slope = logistic * (1.0 + b * (1.0 - logistic)) * v
        slope_normed = slope * normed
        im_ref[0, 0] = image_sum(du * h)
        im_ref[0, 1] = image_sum(du * slope)
        im_ref[0, 2] = image_sum(du * slope_normed)
        im_ref[0, 3] = image_sum(slope)
        im_ref[0, 4] = image_sum(slope_normed)


def third_backward(a3, x, og, p, v, den, l, c, p2, gate):
    rows = x.shape[0]
    images = rows // PIX
    steps = images // IMGS
    part = IMGS * PIX
    first = lambda i: jnp.minimum(i, steps - 1)
    then = lambda i: jnp.maximum(i - steps, 0)
    return pl.pallas_call(
        third_back_kernel,
        grid=(steps + NB,),
        in_specs=[
            pl.BlockSpec((part, W), lambda i: (first(i), 0)),
            pl.BlockSpec((part, W), lambda i: (first(i), 0)),
            pl.BlockSpec((part, W), lambda i: (first(i), 0)),
            pl.BlockSpec((8, W), lambda i: (0, 0)),
            pl.BlockSpec((part, 1), lambda i: (first(i), 0)),
            pl.BlockSpec((1, IMGS, W), lambda i: (first(i), 0, 0)),
            pl.BlockSpec((W, SP), lambda i: (0, then(i))),
            pl.BlockSpec((rows, SP), lambda i: (0, then(i))),
            pl.BlockSpec((8, SP), lambda i: (0, then(i))),
            pl.BlockSpec((rows, 1), lambda i: (0, 0)),
            pl.BlockSpec((1, images, SP), lambda i: (then(i), 0, 0)),
        ],
        out_specs=[
            pl.BlockSpec((part, W), lambda i: (first(i), 0)),
            pl.BlockSpec((W, SP), lambda i: (0, then(i))),
            pl.BlockSpec((rows, SP), lambda i: (0, then(i))),
            pl.BlockSpec((1, 5, images, SP), lambda i: (then(i), 0, 0, 0)),
        ],
        out_shape=[
            jax.ShapeDtypeStruct((rows, W), f32),
            jax.ShapeDtypeStruct((W, WP), bf16),
            jax.ShapeDtypeStruct((rows, WP), f32),
            jax.ShapeDtypeStruct((NB, 5, images, SP), f32),
        ],
        scratch_shapes=[pltpu.VMEM((rows, W), bf16), pltpu.VMEM((W, rows), bf16)],
        compiler_params=params(56),
        cost_estimate=cost(4 * rows * W * WP, 64 * MiB),
        name="third_backward",
    )(a3, x, og, p, v, den.reshape(steps, IMGS, W), l, c, p2, v, gate)


def excite_back_kernel(
    im_ref, gate_ref, zp_ref, z_ref, sp_ref, qe_ref, ninv_ref,
    pgn_ref, sums_ref, gqb_ref, gqe_ref,
):
    zp = zp_ref[...]
    logistic = sigmoid(zp)
    dz = jnp.zeros(zp.shape, f32)
    deps = []
    for j in range(NB):
        gate = gate_ref[j]
        dep = (im_ref[j, 0] * gate * (1.0 - gate)).astype(bf16)
        deps.append(dep)
        dz = dz + nn(dep[:, :SB], qe_ref[j * SB : (j + 1) * SB, RP:])
    dzp = (dz * (logistic * (1.0 + zp * (1.0 - logistic)))).astype(bf16)
    gqb_ref[...] = jnp.sum(dzp.astype(f32), axis=0, keepdims=True)
    pgn_ref[...] = jnp.zeros_like(pgn_ref)
    for j in range(NB):
        rows = slice(j * SB, (j + 1) * SB)
        pgn_ref[j, :, :SB] = nt(dzp, qe_ref[rows, :RP]) * ninv_ref[...]
        pgn = pgn_ref[j]
        gate = gate_ref[j]
        sums_ref[j, 0:1, :] = jnp.sum(
            gate * im_ref[j, 2] + pgn * im_ref[j, 4], axis=0, keepdims=True
        )
        sums_ref[j, 1:2, :] = jnp.sum(
            gate * im_ref[j, 1] + pgn * im_ref[j, 3], axis=0, keepdims=True
        )
        dep = deps[j]
        sums_ref[j, 2:3, :] = jnp.sum(dep.astype(f32), axis=0, keepdims=True)
        gqe_ref[rows, :RP] = tn(sp_ref[j], dzp)[:SB].astype(bf16)
        gqe_ref[rows, RP:] = tn(dep, z_ref[...])[:SB].astype(bf16)


def excite_backward(im, gate, zp, z, sp, qe, ninv):
    images = zp.shape[0]
    return pl.pallas_call(
        excite_back_kernel,
        out_shape=[
            jax.ShapeDtypeStruct((NB, images, SP), f32),
            jax.ShapeDtypeStruct((NB, 3, SP), f32),
            jax.ShapeDtypeStruct((1, RP), f32),
            jax.ShapeDtypeStruct((W, 2 * RP), bf16),
        ],
        compiler_params=params(40),
        cost_estimate=cost(8 * images * W * RP, 10 * MiB),
        name="excite_backward",
    )(im, gate, zp, z, sp, qe, ninv)


def conv_back_kernel(
    a_ref, c_ref, du_ref, p1_ref, p2_ref, v_ref, gate_ref, pgn_ref, k_ref,
    db_ref, gk_ref, st_ref,
    taps, w_scr,
):
    v = v_ref[...]
    rows = v.shape[0]
    normed = (c_ref[...] - p2_ref[0:1, :]) * p2_ref[1:2, :]
    b = p2_ref[2:3, :] * normed + p2_ref[3:4, :]
    logistic = sigmoid(b)
    slope = logistic * (1.0 + b * (1.0 - logistic)) * v
    dh = du_ref[...] * over_pixels(gate_ref[0], rows) + over_pixels(pgn_ref[0], rows)
    dc = v * p2_ref[4:5, :] * (dh * slope - (p2_ref[5:6, :] + normed * p2_ref[6:7, :]))
    spread_taps(dc, taps, -1)
    build_blocks(k_ref, w_scr)
    normed = (a_ref[...] - p1_ref[0:1, :]) * p1_ref[1:2, :]
    b = p1_ref[2:3, :] * normed + p1_ref[3:4, :]
    logistic = sigmoid(b)
    slope = logistic * (1.0 + b * (1.0 - logistic)) * v
    h = (b * logistic * v).astype(bf16)
    grads = tn(h, taps[...])
    mask = block_mask()
    copies = lane_copies()
    for tap in range(9):
        part = jnp.where(mask, grads[:SB, tap * SP : (tap + 1) * SP], 0.0).astype(bf16)
        small = nt(part, copies)
        for q in range(4):
            gk_ref[q, tap] = small[q * GW : (q + 1) * GW].astype(bf16)
    dh1 = jnp.zeros((rows, SP), f32)
    for tap in range(9):
        cols = slice(tap * SP, (tap + 1) * SP)
        dh1 = dh1 + nt(taps[:, cols], w_scr[cols, :])
    db = dh1 * slope
    db_ref[...] = db
    st_ref[0:1, :] = jnp.sum(db * normed, axis=0, keepdims=True)
    st_ref[1:2, :] = jnp.sum(db, axis=0, keepdims=True)


def conv_backward(a, c, du, p1, p2, v, gate, pgn, k):
    rows = a.shape[0]
    images = rows // PIX
    wide = pl.BlockSpec((rows, SP), lambda j: (0, j))
    vec = pl.BlockSpec((8, SP), lambda j: (0, j))
    img = pl.BlockSpec((1, images, SP), lambda j: (j, 0, 0))
    return pl.pallas_call(
        conv_back_kernel,
        grid=(NB,),
        in_specs=[
            wide, wide, wide, vec, vec,
            pl.BlockSpec((rows, 1), lambda j: (0, 0)),
            img, img,
            pl.BlockSpec((4, 9, GW, GW), lambda j: (j, 0, 0, 0)),
        ],
        out_specs=[
            wide,
            pl.BlockSpec((4, 9, GW, GW), lambda j: (j, 0, 0, 0)),
            pl.BlockSpec((2, SP), lambda j: (0, j)),
        ],
        out_shape=[
            jax.ShapeDtypeStruct((rows, WP), f32),
            jax.ShapeDtypeStruct((W // GW, 9, GW, GW), bf16),
            jax.ShapeDtypeStruct((2, WP), f32),
        ],
        scratch_shapes=[pltpu.VMEM((rows, 9 * SP), bf16), pltpu.VMEM((9 * SP, SP), bf16)],
        compiler_params=params(56),
        cost_estimate=cost(4 * rows * 9 * SP * WP, 48 * MiB),
        name="conv_backward",
    )(a, c, du, p1, p2, v, gate, pgn, k)


def first_back_kernel(a_ref, db_ref, p_ref, v_ref, x_ref, da_ref, gf_ref):
    normed = (a_ref[...] - p_ref[0:1, :]) * p_ref[1:2, :]
    da = v_ref[...] * p_ref[4:5, :] * (db_ref[...] - (p_ref[5:6, :] + normed * p_ref[6:7, :]))
    low = da.astype(bf16)
    da_ref[...] = low
    gf_ref[...] = tn(low, x_ref[...])[:SB].astype(bf16)


def first_backward(a, db, p, v, x):
    rows = a.shape[0]
    wide = pl.BlockSpec((rows, SP), lambda j: (0, j))
    return pl.pallas_call(
        first_back_kernel,
        grid=(NB,),
        in_specs=[
            wide,
            wide,
            pl.BlockSpec((8, SP), lambda j: (0, j)),
            pl.BlockSpec((rows, 1), lambda j: (0, 0)),
            pl.BlockSpec((rows, W), lambda j: (0, 0)),
        ],
        out_specs=[wide, pl.BlockSpec((SB, W), lambda j: (j, 0))],
        out_shape=[
            jax.ShapeDtypeStruct((rows, WP), bf16),
            jax.ShapeDtypeStruct((W, W), bf16),
        ],
        compiler_params=params(48),
        cost_estimate=cost(2 * rows * W * WP, 36 * MiB),
        name="first_backward",
    )(a, db, p, v, x)


def input_grad_kernel(da_ref, f_ref, dv_ref, out_ref):
    total = dv_ref[...]
    for j in range(NB):
        total = total + nn(
            da_ref[:, j * SP : j * SP + SB], f_ref[j * SB : (j + 1) * SB, :]
        )
    out_ref[...] = total


def input_gradient(da, f, dv):
    rows = da.shape[0]
    return pl.pallas_call(
        input_grad_kernel,
        grid=(pl.cdiv(W, SP),),
        in_specs=[
            pl.BlockSpec((rows, WP), lambda j: (0, 0)),
            pl.BlockSpec((W, SP), lambda j: (0, j)),
            pl.BlockSpec((rows, SP), lambda j: (0, j)),
        ],
        out_specs=pl.BlockSpec((rows, SP), lambda j: (0, j)),
        out_shape=jax.ShapeDtypeStruct((rows, W), f32),
        compiler_params=params(40),
        cost_estimate=cost(2 * rows * W * WP, 32 * MiB),
        name="input_gradient",
    )(da, f, dv)


def exchanges(value, combine):
    value = combine(value, lax.ppermute(value, "crop", [(0, 1), (1, 0)]))
    count = lax.axis_size("pix")
    step = 1
    while step < count:
        pairs = [(i, i ^ step) for i in range(count)]
        value = combine(value, lax.ppermute(value, "pix", pairs))
        step *= 2
    return value


def add_all(value):
    return exchanges(value, lambda a, b: a + b)


def join_moments(a, b):
    n = a[2] + b[2]
    gap = b[0] - a[0]
    mean = (a[2] * a[0] + b[2] * b[0]) / n
    squares = (a[1] + b[1]) + gap * gap * (a[2] * b[2] / n)
    return jnp.stack([mean, squares, n])


def moments_all(stats, count):
    full = jnp.concatenate([stats, jnp.full((1, stats.shape[1]), count)], axis=0)
    full = exchanges(full, join_moments)
    inverse = lax.rsqrt(full[1] / full[2] + epsilon_norm)
    return full[0], inverse, full[2, 0]


def pad_channels(vec):
    lead = vec.shape[:-1]
    blocks = vec.reshape(lead + (NB, SB))
    return jnp.pad(blocks, [(0, 0)] * len(lead) + [(0, 0), (0, SP - SB)]).reshape(lead + (WP,))


def cut_channels(vec):
    lead = vec.shape[:-1]
    return vec.reshape(lead + (NB, SP))[..., :SB].reshape(lead + (W,))


def rows_of(*vectors):
    block = jnp.stack(vectors)
    return jnp.pad(block, ((0, 8 - len(vectors)), (0, 0)))


def pad_last(block):
    rows = block.shape[0]
    return jnp.pad(block.reshape(rows, NB, SB), ((0, 0), (0, 0), (0, SP - SB))).reshape(rows, WP)


def cut_last(block):
    rows = block.shape[0]
    return block.reshape(rows, NB, SP)[:, :, :SB].reshape(rows, W)


def split_packed(packed):
    half = W // 2
    kernel_end = W + 9 * GW // 2
    edges = (0, half, W, kernel_end, kernel_end + R // 2, packed.shape[1])
    return [packed[:, a:b] for a, b in zip(edges[:-1], edges[1:])]


def pad_units(squeeze, excite):
    wide = ((0, 0), (0, RP - R))
    return jnp.concatenate([jnp.pad(squeeze, wide), jnp.pad(excite, wide)], axis=1)


def aligned(rows):
    return rows % 4 == 0


def gather_weights(packed):
    rows = packed.shape[0]
    blocks = split_packed(packed.astype(bf16))
    if not aligned(rows):
        whole = [lax.all_gather(b, "pix", axis=0, tiled=True) for b in blocks]
        first, third, squeeze, excite = (
            whole[i].reshape(W, -1) for i in (0, 1, 3, 4)
        )
        kernel = whole[2].reshape(W // GW, 9, GW, GW)
        return first, pad_last(third), kernel, pad_units(squeeze, excite)
    mine = lax.axis_index("crop")

    def gather(block):
        share = block.shape[0] // 2
        block = lax.dynamic_slice_in_dim(block, mine * share, share, 0)
        return lax.all_gather(block, ("pix", "crop"), axis=0, tiled=True)

    first = gather(blocks[0].reshape(rows // 2, W))
    kernel = gather(blocks[2].reshape(-1, GW)).reshape(W // GW, 9, GW, GW)
    units = gather(
        pad_units(blocks[3].reshape(rows // 2, R), blocks[4].reshape(rows // 2, R))
    )
    third = gather(pad_last(blocks[1].reshape(rows // 2, W)))
    return first, third, kernel, units


def scatter_gradient(block, rows):
    parts = lax.axis_size("pix") * lax.axis_size("crop")
    share = block.reshape((parts, block.shape[0] // parts) + block.shape[1:])
    return lax.psum_scatter(share, ("pix", "crop"), scatter_dimension=0, tiled=False)


def adam_step(parameter, gradient, first_moment, second_moment, step_rate, decay_rate):
    first_new = beta_one * first_moment + (1.0 - beta_one) * gradient
    second_new = beta_two * second_moment + (1.0 - beta_two) * gradient * gradient
    corrected = (
        first_new
        / (1.0 - beta_one**STEP)
        / (jnp.sqrt(second_new / (1.0 - beta_two**STEP)) + adam_epsilon)
    )
    return (parameter - step_rate * (corrected + decay_rate * parameter), first_new, second_new)


def reduce_gradients(gf, gl, gk, gqe, rows):
    if not aligned(rows):
        packed_grad = jnp.concatenate(
            [
                gf.reshape(2 * W, W // 2),
                cut_last(gl).reshape(2 * W, W // 2),
                gk.reshape(2 * W, 9 * GW // 2),
                gqe[:, :R].reshape(2 * W, R // 2),
                gqe[:, RP : RP + R].reshape(2 * W, R // 2),
            ],
            axis=1,
        )
        owned = lax.psum_scatter(packed_grad, "pix", scatter_dimension=0, tiled=True)
        owned = lax.psum(owned, "crop").astype(f32)
        return owned, lax.psum(jnp.sum(owned * owned), "pix")
    halves = [
        scatter_gradient(block, rows) for block in (gf, gl, gk.reshape(-1, GW), gqe)
    ]
    squared = sum(jnp.sum(jnp.square(h.astype(f32))) for h in halves)
    squared = add_all(jnp.full((8, 128), squared))[0, 0]
    gf, gl, gk, gqe = (lax.all_gather(h, "crop", axis=0, tiled=True) for h in halves)
    owned = jnp.concatenate(
        [
            gf.reshape(rows, W // 2),
            cut_last(gl).reshape(rows, W // 2),
            gk.reshape(rows, 9 * GW // 2),
            gqe[:, :R].reshape(rows, R // 2),
            gqe[:, RP : RP + R].reshape(rows, R // 2),
        ],
        axis=1,
    )
    return owned.astype(f32), squared


def local(
    inputs,
    out_grad,
    pixel_mask,
    crop_source,
    packed,
    moment_one,
    moment_two,
    vector,
    vector_one,
    vector_two,
):
    images = inputs.shape[1]
    rows = images * PIX
    total_images = images * lax.axis_size("pix")
    x = inputs.reshape(rows, W)
    og = out_grad.reshape(rows, W)
    mask = pixel_mask.reshape(images, PIX).astype(f32)
    v = mask.reshape(rows, 1)
    ninv = 1.0 / jnp.sum(mask, axis=1)[:, None]
    local_count = jnp.sum(mask)
    crop = lax.axis_index("crop")
    pix = lax.axis_index("pix")

    gains = vector[: 3 * W].reshape(3, W)
    shifts = vector[3 * W : 6 * W].reshape(3, W)
    gains_wide = pad_channels(gains)
    shifts_wide = pad_channels(shifts)
    eb = pad_channels(vector[6 * W : 7 * W]).reshape(NB, 1, SP)
    qb = jnp.pad(vector[7 * W :], (0, RP - R))[None, :]

    first, third, kernel, units = gather_weights(packed)
    sources = lax.all_gather(crop_source, "pix", axis=0, tiled=True)
    every = jnp.arange(total_images, dtype=jnp.int32)
    counts = jnp.sum((sources[:, None] == every[None, :]).astype(f32), axis=0)
    mine = pix * images + jnp.arange(images, dtype=jnp.int32)
    hits = jnp.where(
        crop == 1, crop_source[:, None] == every[None, :], mine[:, None] == sources[None, :]
    ).astype(bf16)
    wanted = jnp.where(crop == 1, crop_source, mine)
    divisor = jnp.sum((wanted[:, None] == every[None, :]).astype(f32) * counts[None, :], axis=1)
    align = (align_weight / jnp.maximum(divisor, 1.0))[:, None]

    a1, stats = first_matmul(x, first, v)
    mean1, inv1, n = moments_all(stats, local_count)
    fwd1 = rows_of(mean1, inv1 * gains_wide[0], shifts_wide[0])
    c, stats = conv_forward(a1, fwd1, v, kernel)
    mean2, inv2, _ = moments_all(stats, local_count)
    fwd2 = rows_of(mean2, inv2 * gains_wide[1], shifts_wide[1])
    a3, stats, sp, zp, z, gate = third_matmul(c, fwd2, v, ninv, units, eb, qb, third)
    mean3, inv3, _ = moments_all(stats, local_count)
    fwd3 = rows_of(mean3, inv3, gains[2], shifts[2])
    output, per_image, og_sums = output_pass(a3, x, og, fwd3, v, ninv)
    per_image = per_image.transpose(1, 0, 2, 3).reshape(3, images, W)

    other = lax.ppermute(per_image[0].astype(bf16), "crop", [(0, 1), (1, 0)])
    others = lax.all_gather(other, "pix", axis=0, tiled=True)
    den = nn(hits, others) * align * ninv

    sums3 = add_all(
        og_sums
        + jnp.stack([jnp.sum(den * per_image[2], axis=0), jnp.sum(den * per_image[1], axis=0)])
    )
    back3 = rows_of(
        mean3, inv3, gains[2], shifts[2], gains[2] * inv3, sums3[1] / n, sums3[0] / n
    )
    fwd2 = rows_of(mean2, inv2, gains_wide[1], shifts_wide[1])
    dv, gl, du, im = third_backward(a3, x, og, back3, v, den, third, c, fwd2, gate)
    pgn, sums2, gqb, gqe = excite_backward(im, gate, zp, z, sp, units, ninv)
    sums2 = sums2.transpose(1, 0, 2).reshape(3, WP)
    sums2 = add_all(jnp.concatenate([sums2, jnp.pad(gqb, ((0, 0), (0, WP - RP)))], axis=0))
    back2 = rows_of(
        mean2, inv2, gains_wide[1], shifts_wide[1], gains_wide[1] * inv2, sums2[1] / n,
        sums2[0] / n,
    )
    fwd1 = rows_of(mean1, inv1, gains_wide[0], shifts_wide[0])
    db1, gk, sums1 = conv_backward(a1, c, du, fwd1, back2, v, gate, pgn, kernel)
    sums1 = add_all(sums1)
    back1 = rows_of(
        mean1, inv1, gains_wide[0], shifts_wide[0], gains_wide[0] * inv1, sums1[1] / n,
        sums1[0] / n,
    )
    da1, gf = first_backward(a1, db1, back1, v, x)
    input_grad = input_gradient(da1, first, dv)

    vector_grad = jnp.concatenate(
        [
            cut_channels(sums1[0]),
            cut_channels(sums2[0]),
            sums3[0],
            cut_channels(sums1[1]),
            cut_channels(sums2[1]),
            sums3[1],
            cut_channels(sums2[2]),
            sums2[3, :R],
        ]
    )
    owned_grad, squared = reduce_gradients(gf, gl, gk, gqe, packed.shape[0])
    grad_norm = jnp.sqrt(squared + jnp.sum(vector_grad * vector_grad))
    factor = jnp.minimum(1.0, clip_bound / (grad_norm + 1e-06))
    packed_new, moment_one_new, moment_two_new = adam_step(
        packed, factor * owned_grad, moment_one, moment_two, rate_matrix, decay_matrix
    )
    vector_new, vector_first, vector_second = adam_step(
        vector, factor * vector_grad, vector_one, vector_two, rate_vector, 0.0
    )
    return (
        output.reshape(inputs.shape),
        input_grad.reshape(inputs.shape),
        packed_new,
        moment_one_new,
        moment_two_new,
        vector_new,
        vector_first,
        vector_second,
        grad_norm,
    )


def solution(mesh):
    in_specs = (
        P("crop", "pix", None, None),
        P("crop", "pix", None, None),
        P("crop", "pix", None),
        P("pix"),
        P("pix", None),
        P("pix", None),
        P("pix", None),
        P(),
        P(),
        P(),
    )
    out_specs = (
        P("crop", "pix", None, None),
        P("crop", "pix", None, None),
        P("pix", None),
        P("pix", None),
        P("pix", None),
        P(),
        P(),
        P(),
        P(),
    )
    return jax.shard_map(local, mesh=mesh, in_specs=in_specs, out_specs=out_specs, check_vma=False)
```

```python
import jax
import jax.numpy as jnp
from jax import lax
from jax.experimental import pallas as pl
from jax.experimental.pallas import tpu as pltpu
from jax.sharding import PartitionSpec as P

W = 2016
GW = 56
R = 504
GRID = 8
PIX = GRID * GRID
STEP = 10
SB = 224
SP = 256
NB = W // SB
WP = NB * SP
RP = 512
OWN = 126
OWNERS = W // OWN
HALF = 64
KP = 512
F_EDGES = (0, 640, 1280, W)
U_EDGES = (0, RP, 2 * RP)

epsilon_norm = 1e-05
align_weight = 16.0
clip_bound = 1.0
beta_one = 0.9
beta_two = 0.999
adam_epsilon = 1e-08
rate_matrix = 0.02
rate_vector = 0.4
decay_matrix = 0.05

f32 = jnp.float32
bf16 = jnp.bfloat16
MiB = 1024 * 1024


def params():
    return pltpu.CompilerParams(vmem_limit_bytes=63 * MiB)


def cost(flops, nbytes, exps=0):
    return pl.CostEstimate(flops=flops, bytes_accessed=nbytes, transcendentals=exps)


def nn(a, b):
    return lax.dot_general(a, b, (((1,), (0,)), ((), ())), preferred_element_type=f32)


def nt(a, b):
    return lax.dot_general(a, b, (((1,), (1,)), ((), ())), preferred_element_type=f32)


def tn(a, b):
    return lax.dot_general(a, b, (((0,), (0,)), ((), ())), preferred_element_type=f32)


def sigmoid(t):
    return 0.5 * jnp.tanh(0.5 * t) + 0.5


def over_pixels(per_image, rows):
    images, width = per_image.shape
    wide = jnp.broadcast_to(per_image[:, None, :], (images, PIX, width))
    return wide.reshape(rows, width)


def fold(values):
    return jnp.sum(values.reshape(values.shape[0] // 8, 8, values.shape[1]), axis=0)


def total_of(values):
    return jnp.sum(values, axis=0, keepdims=True)


def image_rows(i):
    return slice(i * PIX, (i + 1) * PIX)


def valid_rows(v_ref, i, width):
    v = v_ref[image_rows(i), :]
    if width <= 128:
        return v[:, :width]
    return jnp.concatenate([v, v[:, : width - 128]], axis=1)


def over_images(images, body, init):
    for i in range(images):
        init = body(i, init)
    return init


def block_moments(a_ref, v_ref, st_ref, width):
    images = a_ref.shape[0] // PIX
    lead = min(width, 128)

    def add(i, sums):
        v = valid_rows(v_ref, i, width)
        return sums[0] + fold(a_ref[image_rows(i), :width] * v), sums[1] + fold(v[:, :lead])

    zero = jnp.zeros((8, width), f32)
    sums, counts = over_images(images, add, (zero, jnp.zeros((8, lead), f32)))
    mean = total_of(sums) / total_of(counts)[:, :1]

    def square(i, sums):
        centered = a_ref[image_rows(i), :width] - mean
        return sums + fold(centered * centered * valid_rows(v_ref, i, width))

    st_ref[0:1, :width] = mean
    st_ref[1:2, :width] = total_of(over_images(images, square, zero))


def pieces(start, count):
    out = []
    at = start
    while at < min(start + count, W):
        owner, row = divmod(at, OWN)
        half = row // HALF
        end = min(owner * OWN + (HALF if half == 0 else OWN), start + count, W)
        out.append((owner, half, row - half * HALF, at - start, end - at))
        at = end
    return out


def collect_rows(to_ref, from_ref, start, count):
    for owner, half, row, here, n in pieces(start, count):
        first = half * HALF + row
        to_ref[here : here + n, :] = from_ref[owner, first : first + n, :]


def deal_rows(keep_refs, send_refs, edges, from_ref, start, count, crop):
    for owner, half, row, here, n in pieces(start, count):
        for keep, send, a, b in zip(keep_refs, send_refs, edges[:-1], edges[1:]):

            @pl.when(crop == half)
            def _():
                keep[owner, row : row + n, :] = from_ref[here : here + n, a:b].astype(bf16)

            @pl.when(crop != half)
            def _():
                send[owner, row : row + n, :] = from_ref[here : here + n, a:b].astype(bf16)


def clear_padding(refs):
    for ref in refs:
        for owner in range(OWNERS):
            ref[owner, OWN - HALF :, :] = jnp.zeros((2 * HALF - OWN, ref.shape[2]), bf16)


def at_step(step, count, body):
    for j in range(count):

        @pl.when(step == j)
        def _():
            body(j)


def dealt_shapes(edges):
    return [
        jax.ShapeDtypeStruct((OWNERS, HALF, b - a), bf16) for a, b in zip(edges[:-1], edges[1:])
    ] * 2


def dealt_specs(edges):
    return [
        pl.BlockSpec((OWNERS, HALF, b - a), lambda *_: (0, 0, 0))
        for a, b in zip(edges[:-1], edges[1:])
    ] * 2


SCALAR = pl.BlockSpec(memory_space=pltpu.SMEM)


def first_kernel(x_ref, own_ref, v_ref, a_ref, st_ref, f_ref):
    at_step(pl.program_id(0), NB, lambda j: collect_rows(f_ref, own_ref, j * SB, SB))
    a_ref[:, :SB] = nt(x_ref[...], f_ref[...])
    a_ref[:, SB:] = jnp.zeros((a_ref.shape[0], SP - SB), f32)
    st_ref[...] = jnp.zeros_like(st_ref)
    block_moments(a_ref, v_ref, st_ref, SB)


def first_matmul(x, own, v):
    rows = x.shape[0]
    return pl.pallas_call(
        first_kernel,
        grid=(NB,),
        in_specs=[
            pl.BlockSpec((rows, W), lambda j: (0, 0)),
            pl.BlockSpec((OWNERS, 2 * HALF, W), lambda j: (0, 0, 0)),
            pl.BlockSpec((rows, 128), lambda j: (0, 0)),
        ],
        out_specs=[
            pl.BlockSpec((rows, SP), lambda j: (0, j)),
            pl.BlockSpec((2, SP), lambda j: (0, j)),
            pl.BlockSpec((SB, W), lambda j: (j, 0)),
        ],
        out_shape=[
            jax.ShapeDtypeStruct((rows, WP), f32),
            jax.ShapeDtypeStruct((2, WP), f32),
            jax.ShapeDtypeStruct((W, W), bf16),
        ],
        compiler_params=params(),
        cost_estimate=cost(2 * rows * W * WP, 32 * MiB),
        name="first_matmul",
    )(x, own, v)


def shifted(values, row_step, col_step, sub):
    rows, width = values.shape
    if col_step == -1:
        values = jnp.where(sub == 0, 0.0, pltpu.roll(values, 1, 0))
    elif col_step == 1:
        values = jnp.where(sub == GRID - 1, 0.0, pltpu.roll(values, rows - 1, 0))
    if row_step:
        grid = values.reshape(rows // PIX, PIX, width)
        edge = jnp.zeros((rows // PIX, GRID, width), values.dtype)
        if row_step == -1:
            grid = jnp.concatenate([edge, grid[:, : PIX - GRID]], axis=1)
        else:
            grid = jnp.concatenate([grid[:, GRID:], edge], axis=1)
        values = grid.reshape(rows, width)
    return values


def spread_taps(values, scratch, sign, i):
    sub = lax.broadcasted_iota(jnp.int32, values.shape, 0) & (GRID - 1)
    for dx in range(3):
        moved = shifted(values, 0, sign * (dx - 1), sub)
        for dy in range(3):
            tap = 3 * dy + dx
            scratch[image_rows(i), tap * SP : (tap + 1) * SP] = shifted(
                moved, sign * (dy - 1), 0, sub
            ).astype(bf16)


def group_of(shape, axis):
    at = lax.broadcasted_iota(jnp.int32, shape, axis)
    return (
        (at >= GW).astype(jnp.int32)
        + (at >= 2 * GW).astype(jnp.int32)
        + (at >= 3 * GW).astype(jnp.int32)
        + (at >= 4 * GW).astype(jnp.int32)
    )


def lane_copies():
    out = lax.broadcasted_iota(jnp.int32, (GW, SP), 0)
    lane = lax.broadcasted_iota(jnp.int32, (GW, SP), 1)
    within = lane - GW * group_of((GW, SP), 1)
    return ((within == out) & (lane < SB)).astype(f32).astype(bf16)


def block_mask():
    return group_of((SB, SP), 0) == group_of((SB, SP), 1)


def build_blocks(k_ref, w_scr, k_scr):
    copies = lane_copies()
    mask = block_mask()
    packed = k_ref[...].astype(f32)
    for q in range(4):
        for m in range(9):
            k_scr[pl.ds(9 * GW * q + m, GW, stride=9), :] = packed[
                q * GW : (q + 1) * GW, m * GW : (m + 1) * GW
            ]
    for tap in range(9):
        starts = [9 * GW * q + GW * tap for q in range(4)]
        stack = jnp.concatenate([k_scr[a : a + GW, :] for a in starts], axis=0)
        wide = nn(stack.astype(bf16), copies)
        w_scr[tap * SP : tap * SP + SB, :] = jnp.where(mask, wide, 0.0).astype(bf16)
        w_scr[tap * SP + SB : (tap + 1) * SP, :] = jnp.zeros((SP - SB, SP), bf16)


def conv_kernel(a_ref, p_ref, v_ref, k_ref, c_ref, st_ref, taps, w_scr, k_scr):
    images = a_ref.shape[0] // PIX

    def activate(i, _):
        b = (a_ref[image_rows(i), :] - p_ref[0:1, :]) * p_ref[1:2, :] + p_ref[2:3, :]
        spread_taps(b * sigmoid(b) * valid_rows(v_ref, i, SP), taps, 1, i)
        return 0

    over_images(images, activate, 0)
    build_blocks(k_ref, w_scr, k_scr)
    c_ref[...] = nn(taps[...], w_scr[...])
    block_moments(c_ref, v_ref, st_ref, SP)


def conv_forward(a, p, v, k):
    rows = a.shape[0]
    return pl.pallas_call(
        conv_kernel,
        grid=(NB,),
        in_specs=[
            pl.BlockSpec((rows, SP), lambda j: (0, j)),
            pl.BlockSpec((8, SP), lambda j: (0, j)),
            pl.BlockSpec((rows, 128), lambda j: (0, 0)),
            pl.BlockSpec((SB, KP), lambda j: (j, 0)),
        ],
        out_specs=[
            pl.BlockSpec((rows, SP), lambda j: (0, j)),
            pl.BlockSpec((2, SP), lambda j: (0, j)),
        ],
        out_shape=[
            jax.ShapeDtypeStruct((rows, WP), f32),
            jax.ShapeDtypeStruct((2, WP), f32),
        ],
        scratch_shapes=[
            pltpu.VMEM((rows, 9 * SP), bf16),
            pltpu.VMEM((9 * SP, SP), bf16),
            pltpu.VMEM((36 * GW, GW), f32),
        ],
        compiler_params=params(),
        cost_estimate=cost(2 * rows * 9 * SP * WP, 24 * MiB),
        name="conv_forward",
    )(a, p, v, k)


def third_kernel(
    c_ref, p_ref, v_ref, ninv_ref, qe_ref, eb_ref, qb_ref, own_ref,
    a3_ref, st_ref, sp_ref, zp_ref, z_ref, gate_ref, l_ref,
    h2_scr, e_scr, u_scr, sum_scr,
):
    step = pl.program_id(0)
    images = v_ref.shape[0] // PIX

    @pl.when(step == 0)
    def _():
        zp_ref[...] = jnp.broadcast_to(qb_ref[...], zp_ref.shape)

    @pl.when(step < NB)
    def _():
        def activate(i, _):
            b = (c_ref[image_rows(i), :] - p_ref[0:1, :]) * p_ref[1:2, :] + p_ref[2:3, :]
            h = b * sigmoid(b) * valid_rows(v_ref, i, SP)
            h2_scr[step, image_rows(i), :] = h
            sum_scr[slice(i, i + 1), :] = total_of(h)
            return 0

        over_images(images, activate, 0)
        pooled = (sum_scr[...] * ninv_ref[...]).astype(bf16)
        sp_ref[step] = pooled
        zp_ref[...] += nn(pooled[:, :SB], qe_ref[:, :RP])
        e_scr[step] = qe_ref[:, RP:]

    @pl.when(step == NB)
    def _():
        zp = zp_ref[...]
        z = (zp * sigmoid(zp)).astype(bf16)
        z_ref[...] = z
        gate_ref[...] = jnp.zeros_like(gate_ref)
        for j in range(NB):
            gate_ref[j, :, :SB] = sigmoid(nt(z, e_scr[j]) + eb_ref[j, :, :SB])

            def scale(i, _):
                u = h2_scr[j, image_rows(i), :] * gate_ref[j, slice(i, i + 1), :]
                u_scr[image_rows(i), j * SP : (j + 1) * SP] = u.astype(bf16)
                return 0

            over_images(images, scale, 0)

    @pl.when(step >= NB)
    def _():
        at_step(
            step - NB, pl.cdiv(W, SP), lambda k: collect_rows(l_ref, own_ref, k * SP, SP)
        )
        a3_ref[...] = nt(u_scr[...], l_ref[...])
        block_moments(a3_ref, v_ref, st_ref, SP)


def third_matmul(c, p, v, ninv, qe, eb, qb, own):
    rows = c.shape[0]
    images = rows // PIX
    first = lambda i: jnp.minimum(i, NB - 1)
    then = lambda i: jnp.maximum(i - NB, 0)
    blocks = pl.cdiv(W, SP)
    return pl.pallas_call(
        third_kernel,
        grid=(NB + blocks,),
        in_specs=[
            pl.BlockSpec((rows, SP), lambda i: (0, first(i))),
            pl.BlockSpec((8, SP), lambda i: (0, first(i))),
            pl.BlockSpec((rows, 128), lambda i: (0, 0)),
            pl.BlockSpec((images, 1), lambda i: (0, 0)),
            pl.BlockSpec((SB, 2 * RP), lambda i: (first(i), 0)),
            pl.BlockSpec((NB, 1, SP), lambda i: (0, 0, 0)),
            pl.BlockSpec((1, RP), lambda i: (0, 0)),
            pl.BlockSpec((OWNERS, 2 * HALF, WP), lambda i: (0, 0, 0)),
        ],
        out_specs=[
            pl.BlockSpec((rows, SP), lambda i: (0, then(i))),
            pl.BlockSpec((2, SP), lambda i: (0, then(i))),
            pl.BlockSpec((NB, images, SP), lambda i: (0, 0, 0)),
            pl.BlockSpec((images, RP), lambda i: (0, 0)),
            pl.BlockSpec((images, RP), lambda i: (0, 0)),
            pl.BlockSpec((NB, images, SP), lambda i: (0, 0, 0)),
            pl.BlockSpec((SP, WP), lambda i: (then(i), 0)),
        ],
        out_shape=[
            jax.ShapeDtypeStruct((rows, W), f32),
            jax.ShapeDtypeStruct((2, W), f32),
            jax.ShapeDtypeStruct((NB, images, SP), bf16),
            jax.ShapeDtypeStruct((images, RP), f32),
            jax.ShapeDtypeStruct((images, RP), bf16),
            jax.ShapeDtypeStruct((NB, images, SP), f32),
            jax.ShapeDtypeStruct((W, WP), bf16),
        ],
        scratch_shapes=[
            pltpu.VMEM((NB, rows, SP), f32),
            pltpu.VMEM((NB, SB, RP), bf16),
            pltpu.VMEM((rows, WP), bf16),
            pltpu.VMEM((images, SP), f32),
        ],
        compiler_params=params(),
        cost_estimate=cost(2 * rows * W * WP, 32 * MiB),
        name="third_matmul",
    )(c, p, v, ninv, qe, eb, qb, own)


IMGS = 4


def lane_blocks(width):
    return [slice(a, min(a + SP, width)) for a in range(0, width, SP)]


def output_kernel(a3_ref, x_ref, og_ref, p_ref, v_ref, ninv_ref, out_ref, im_ref, t_ref):
    step = pl.program_id(0)

    @pl.when(step == 0)
    def _():
        t_ref[...] = jnp.zeros_like(t_ref)

    for cols in lane_blocks(W):
        width = cols.stop - cols.start

        def image(i, sums):
            rows = image_rows(i)
            v = valid_rows(v_ref, i, width)
            normed = (a3_ref[rows, cols] - p_ref[0:1, cols]) * p_ref[1:2, cols]
            total = p_ref[2:3, cols] * normed + p_ref[3:4, cols] + x_ref[rows, cols].astype(f32)
            logistic = sigmoid(total)
            out = total * logistic * v
            out_ref[rows, cols] = out.astype(bf16)
            slope = logistic * (1.0 + total * (1.0 - logistic)) * v
            slope_normed = slope * normed
            og = og_ref[rows, cols].astype(f32)
            im_ref[0, 0, slice(i, i + 1), cols] = total_of(out)
            im_ref[0, 1, slice(i, i + 1), cols] = total_of(slope)
            im_ref[0, 2, slice(i, i + 1), cols] = total_of(slope_normed)
            return sums[0] + fold(og * slope_normed), sums[1] + fold(og * slope)

        zero = jnp.zeros((8, width), f32)
        one, two = over_images(IMGS, image, (zero, zero))
        t_ref[0:1, cols] += total_of(one)
        t_ref[1:2, cols] += total_of(two)
    im_ref[0, 0] = im_ref[0, 0] * ninv_ref[0]


def output_pass(a3, x, og, p, v, ninv):
    rows = x.shape[0]
    images = rows // PIX
    steps = images // IMGS
    part = IMGS * PIX
    return pl.pallas_call(
        output_kernel,
        grid=(steps,),
        in_specs=[
            pl.BlockSpec((part, W), lambda i: (i, 0)),
            pl.BlockSpec((part, W), lambda i: (i, 0)),
            pl.BlockSpec((part, W), lambda i: (i, 0)),
            pl.BlockSpec((8, W), lambda i: (0, 0)),
            pl.BlockSpec((part, 128), lambda i: (i, 0)),
            pl.BlockSpec((1, IMGS, 1), lambda i: (i, 0, 0)),
        ],
        out_specs=[
            pl.BlockSpec((part, W), lambda i: (i, 0)),
            pl.BlockSpec((1, 3, IMGS, W), lambda i: (i, 0, 0, 0)),
            pl.BlockSpec((2, W), lambda i: (0, 0)),
        ],
        out_shape=[
            jax.ShapeDtypeStruct((rows, W), bf16),
            jax.ShapeDtypeStruct((steps, 3, IMGS, W), f32),
            jax.ShapeDtypeStruct((2, W), f32),
        ],
        compiler_params=params(),
        cost_estimate=cost(30 * rows * W, 24 * MiB, 2 * rows * W),
        name="output_pass",
    )(a3, x, og, p, v, ninv.reshape(steps, IMGS, 1))


def third_back_kernel(
    a3_ref, x_ref, og_ref, p_ref, v_ref, den_ref, l_ref, c_ref, p2_ref, vall_ref, gate_ref,
    dv_ref, gl_ref, du_ref, im_ref,
    da_scr, dat_scr, u_scr, t_scr,
):
    step = pl.program_id(0)
    rows = vall_ref.shape[0]
    part = v_ref.shape[0]
    steps = rows // part

    @pl.when(step < steps)
    def _():
        start = pl.multiple_of(step * part, part)
        for cols in lane_blocks(W):
            width = cols.stop - cols.start

            def image(i, _):
                rows = image_rows(i)
                v = valid_rows(v_ref, i, width)
                normed = (a3_ref[rows, cols] - p_ref[0:1, cols]) * p_ref[1:2, cols]
                total = (
                    p_ref[2:3, cols] * normed + p_ref[3:4, cols] + x_ref[rows, cols].astype(f32)
                )
                logistic = sigmoid(total)
                slope = logistic * (1.0 + total * (1.0 - logistic)) * v
                dv = (og_ref[rows, cols].astype(f32) + den_ref[0, slice(i, i + 1), cols]) * slope
                dv_ref[rows, cols] = dv
                da = v * p_ref[4:5, cols] * (dv - (p_ref[5:6, cols] + normed * p_ref[6:7, cols]))
                to = pl.ds(pl.multiple_of(start + i * PIX, PIX), PIX)
                da_scr[to, cols] = da.astype(bf16)
                return 0

            over_images(IMGS, image, 0)
        t_scr[...] = da_scr[pl.ds(start, part), :].T
        to = pl.ds(start, part)
        for owner in range(OWNERS):
            first = owner * 2 * HALF
            dat_scr[first : first + OWN, to] = t_scr[owner * OWN : (owner + 1) * OWN, :]
            dat_scr[first + OWN : first + 2 * HALF, to] = jnp.zeros((2 * HALF - OWN, part), bf16)

    @pl.when(step >= steps)
    def _():
        du_ref[...] = nn(da_scr[...], l_ref[...])

        def image(i, _):
            rows = image_rows(i)
            v = valid_rows(vall_ref, i, SP)
            normed = (c_ref[rows, :] - p2_ref[0:1, :]) * p2_ref[1:2, :]
            b = p2_ref[2:3, :] * normed + p2_ref[3:4, :]
            logistic = sigmoid(b)
            h = b * logistic * v
            u_scr[rows, :] = (h * gate_ref[0, slice(i, i + 1), :]).astype(bf16)
            slope = logistic * (1.0 + b * (1.0 - logistic)) * v
            slope_normed = slope * normed
            du = du_ref[rows, :]
            at = slice(i, i + 1)
            im_ref[0, 0, at, :] = total_of(du * h)
            im_ref[0, 1, at, :] = total_of(du * slope)
            im_ref[0, 2, at, :] = total_of(du * slope_normed)
            im_ref[0, 3, at, :] = total_of(slope)
            im_ref[0, 4, at, :] = total_of(slope_normed)
            return 0

        over_images(rows // PIX, image, 0)
        gl_ref[...] = nn(dat_scr[...], u_scr[...]).astype(bf16)


def third_backward(a3, x, og, p, v, den, l, c, p2, gate):
    rows = x.shape[0]
    images = rows // PIX
    steps = images // IMGS
    part = IMGS * PIX
    first = lambda i: jnp.minimum(i, steps - 1)
    then = lambda i: jnp.maximum(i - steps, 0)
    return pl.pallas_call(
        third_back_kernel,
        grid=(steps + NB,),
        in_specs=[
            pl.BlockSpec((part, W), lambda i: (first(i), 0)),
            pl.BlockSpec((part, W), lambda i: (first(i), 0)),
            pl.BlockSpec((part, W), lambda i: (first(i), 0)),
            pl.BlockSpec((8, W), lambda i: (0, 0)),
            pl.BlockSpec((part, 128), lambda i: (first(i), 0)),
            pl.BlockSpec((1, IMGS, W), lambda i: (first(i), 0, 0)),
            pl.BlockSpec((W, SP), lambda i: (0, then(i))),
            pl.BlockSpec((rows, SP), lambda i: (0, then(i))),
            pl.BlockSpec((8, SP), lambda i: (0, then(i))),
            pl.BlockSpec((rows, 128), lambda i: (0, 0)),
            pl.BlockSpec((1, images, SP), lambda i: (then(i), 0, 0)),
        ],
        out_specs=[
            pl.BlockSpec((part, W), lambda i: (first(i), 0)),
            pl.BlockSpec((OWNERS * 2 * HALF, SP), lambda i: (0, then(i))),
            pl.BlockSpec((rows, SP), lambda i: (0, then(i))),
            pl.BlockSpec((1, 5, images, SP), lambda i: (then(i), 0, 0, 0)),
        ],
        out_shape=[
            jax.ShapeDtypeStruct((rows, W), f32),
            jax.ShapeDtypeStruct((OWNERS * 2 * HALF, WP), bf16),
            jax.ShapeDtypeStruct((rows, WP), f32),
            jax.ShapeDtypeStruct((NB, 5, images, SP), f32),
        ],
        scratch_shapes=[
            pltpu.VMEM((rows, W), bf16),
            pltpu.VMEM((OWNERS * 2 * HALF, rows), bf16),
            pltpu.VMEM((rows, SP), bf16),
            pltpu.VMEM((W, part), bf16),
        ],
        compiler_params=params(),
        cost_estimate=cost(4 * rows * W * WP, 64 * MiB),
        name="third_backward",
    )(a3, x, og, p, v, den.reshape(steps, IMGS, W), l, c, p2, v, gate)


def excite_back_kernel(
    crop_ref, im_ref, gate_ref, zp_ref, z_ref, sp_ref, qe_ref, ninv_ref,
    pgn_ref, sums_ref, gqb_ref, keep_q, keep_e, send_q, send_e,
    g_scr,
):
    zp = zp_ref[...]
    logistic = sigmoid(zp)
    dz = jnp.zeros(zp.shape, f32)
    deps = []
    for j in range(NB):
        gate = gate_ref[j]
        dep = (im_ref[j, 0] * gate * (1.0 - gate)).astype(bf16)
        deps.append(dep)
        dz = dz + nn(dep[:, :SB], qe_ref[j * SB : (j + 1) * SB, RP:])
    dzp = (dz * (logistic * (1.0 + zp * (1.0 - logistic)))).astype(bf16)
    gqb_ref[...] = jnp.sum(dzp.astype(f32), axis=0, keepdims=True)
    pgn_ref[...] = jnp.zeros_like(pgn_ref)
    for j in range(NB):
        rows = slice(j * SB, (j + 1) * SB)
        pgn_ref[j, :, :SB] = nt(dzp, qe_ref[rows, :RP]) * ninv_ref[...]
        pgn = pgn_ref[j]
        gate = gate_ref[j]
        sums_ref[j, 0:1, :] = jnp.sum(
            gate * im_ref[j, 2] + pgn * im_ref[j, 4], axis=0, keepdims=True
        )
        sums_ref[j, 1:2, :] = jnp.sum(
            gate * im_ref[j, 1] + pgn * im_ref[j, 3], axis=0, keepdims=True
        )
        dep = deps[j]
        sums_ref[j, 2:3, :] = jnp.sum(dep.astype(f32), axis=0, keepdims=True)
        g_scr[rows, :RP] = tn(sp_ref[j], dzp)[:SB]
        g_scr[rows, RP:] = tn(dep, z_ref[...])[:SB]
    clear_padding((keep_q, keep_e, send_q, send_e))
    deal_rows((keep_q, keep_e), (send_q, send_e), U_EDGES, g_scr, 0, W, crop_ref[0])


def excite_backward(crop, im, gate, zp, z, sp, qe, ninv):
    images = zp.shape[0]
    return pl.pallas_call(
        excite_back_kernel,
        in_specs=[SCALAR] + [pl.BlockSpec(memory_space=pltpu.VMEM)] * 7,
        out_shape=[
            jax.ShapeDtypeStruct((NB, images, SP), f32),
            jax.ShapeDtypeStruct((NB, 3, SP), f32),
            jax.ShapeDtypeStruct((1, RP), f32),
        ]
        + dealt_shapes(U_EDGES),
        scratch_shapes=[pltpu.VMEM((W, 2 * RP), f32)],
        compiler_params=params(),
        cost_estimate=cost(8 * images * W * RP, 10 * MiB),
        name="excite_backward",
    )(crop, im, gate, zp, z, sp, qe, ninv)


def conv_back_kernel(
    crop_ref, a_ref, c_ref, du_ref, p1_ref, p2_ref, v_ref, gate_ref, pgn_ref, k_ref,
    db_ref, st_ref, keep_ref, send_ref,
    taps, w_scr, h_scr, slope_scr, k_scr, g_scr,
):
    images = v_ref.shape[0] // PIX

    def image(i, _):
        rows = image_rows(i)
        at = slice(i, i + 1)
        v = valid_rows(v_ref, i, SP)
        normed = (c_ref[rows, :] - p2_ref[0:1, :]) * p2_ref[1:2, :]
        b = p2_ref[2:3, :] * normed + p2_ref[3:4, :]
        logistic = sigmoid(b)
        slope = logistic * (1.0 + b * (1.0 - logistic)) * v
        dh = du_ref[rows, :] * gate_ref[0, at, :] + pgn_ref[0, at, :]
        dc = v * p2_ref[4:5, :] * (dh * slope - (p2_ref[5:6, :] + normed * p2_ref[6:7, :]))
        spread_taps(dc, taps, -1, i)
        normed = (a_ref[rows, :] - p1_ref[0:1, :]) * p1_ref[1:2, :]
        b = p1_ref[2:3, :] * normed + p1_ref[3:4, :]
        logistic = sigmoid(b)
        slope_scr[rows, :] = logistic * (1.0 + b * (1.0 - logistic)) * v
        h_scr[rows, :] = (b * logistic * v).astype(bf16)
        return 0

    over_images(images, image, 0)
    build_blocks(k_ref, w_scr, k_scr)
    grads = tn(h_scr[...], taps[...])
    mask = block_mask()
    copies = lane_copies()
    for tap in range(9):
        part = jnp.where(mask, grads[:SB, tap * SP : (tap + 1) * SP], 0.0).astype(bf16)
        small = nt(part, copies)
        for q in range(4):
            first = 9 * GW * q + GW * tap
            k_scr[first : first + GW, :] = small[q * GW : (q + 1) * GW]
    for q in range(4):
        for m in range(9):
            g_scr[q * GW : (q + 1) * GW, m * GW : (m + 1) * GW] = k_scr[
                pl.ds(9 * GW * q + m, GW, stride=9), :
            ]
    step = pl.program_id(0)

    @pl.when(step == 0)
    def _():
        clear_padding((keep_ref, send_ref))

    at_step(
        step,
        NB,
        lambda j: deal_rows(
            (keep_ref,), (send_ref,), (0, KP), g_scr, j * SB, SB, crop_ref[0]
        ),
    )
    dh1 = nt(taps[:, :SP], w_scr[:SP, :])
    for tap in range(1, 9):
        cols = slice(tap * SP, (tap + 1) * SP)
        dh1 = dh1 + nt(taps[:, cols], w_scr[cols, :])
    db_ref[...] = dh1

    def finish(i, sums):
        rows = image_rows(i)
        db = db_ref[rows, :] * slope_scr[rows, :]
        db_ref[rows, :] = db
        normed = (a_ref[rows, :] - p1_ref[0:1, :]) * p1_ref[1:2, :]
        return sums[0] + fold(db * normed), sums[1] + fold(db)

    zero = jnp.zeros((8, SP), f32)
    one, two = over_images(images, finish, (zero, zero))
    st_ref[0:1, :] = total_of(one)
    st_ref[1:2, :] = total_of(two)


def conv_backward(crop, a, c, du, p1, p2, v, gate, pgn, k):
    rows = a.shape[0]
    images = rows // PIX
    wide = pl.BlockSpec((rows, SP), lambda j: (0, j))
    vec = pl.BlockSpec((8, SP), lambda j: (0, j))
    img = pl.BlockSpec((1, images, SP), lambda j: (j, 0, 0))
    return pl.pallas_call(
        conv_back_kernel,
        grid=(NB,),
        in_specs=[
            SCALAR, wide, wide, wide, vec, vec,
            pl.BlockSpec((rows, 128), lambda j: (0, 0)),
            img, img,
            pl.BlockSpec((SB, KP), lambda j: (j, 0)),
        ],
        out_specs=[wide, pl.BlockSpec((2, SP), lambda j: (0, j))] + dealt_specs((0, KP)),
        out_shape=[
            jax.ShapeDtypeStruct((rows, WP), f32),
            jax.ShapeDtypeStruct((2, WP), f32),
        ]
        + dealt_shapes((0, KP)),
        scratch_shapes=[
            pltpu.VMEM((rows, 9 * SP), bf16),
            pltpu.VMEM((9 * SP, SP), bf16),
            pltpu.VMEM((rows, SP), bf16),
            pltpu.VMEM((rows, SP), f32),
            pltpu.VMEM((36 * GW, GW), f32),
            pltpu.VMEM((SB, KP), f32),
        ],
        compiler_params=params(),
        cost_estimate=cost(4 * rows * 9 * SP * WP, 48 * MiB),
        name="conv_backward",
    )(crop, a, c, du, p1, p2, v, gate, pgn, k)


def first_back_kernel(crop_ref, a_ref, db_ref, p_ref, v_ref, x_ref, da_ref, *refs):
    *dealt, g_scr = refs
    half = len(dealt) // 2
    step = pl.program_id(0)

    def image(i, _):
        rows = image_rows(i)
        normed = (a_ref[rows, :] - p_ref[0:1, :]) * p_ref[1:2, :]
        db = db_ref[rows, :] - (p_ref[5:6, :] + normed * p_ref[6:7, :])
        da_ref[rows, :] = (valid_rows(v_ref, i, SP) * p_ref[4:5, :] * db).astype(bf16)
        return 0

    over_images(a_ref.shape[0] // PIX, image, 0)
    g_scr[...] = tn(da_ref[...], x_ref[...])[:SB].astype(bf16)

    @pl.when(step == 0)
    def _():
        clear_padding(dealt)

    at_step(
        step,
        NB,
        lambda j: deal_rows(dealt[:half], dealt[half:], F_EDGES, g_scr, j * SB, SB, crop_ref[0]),
    )


def first_backward(crop, a, db, p, v, x):
    rows = a.shape[0]
    wide = pl.BlockSpec((rows, SP), lambda j: (0, j))
    return pl.pallas_call(
        first_back_kernel,
        grid=(NB,),
        in_specs=[
            SCALAR,
            wide,
            wide,
            pl.BlockSpec((8, SP), lambda j: (0, j)),
            pl.BlockSpec((rows, 128), lambda j: (0, 0)),
            pl.BlockSpec((rows, W), lambda j: (0, 0)),
        ],
        out_specs=[wide] + dealt_specs(F_EDGES),
        out_shape=[jax.ShapeDtypeStruct((rows, WP), bf16)] + dealt_shapes(F_EDGES),
        scratch_shapes=[pltpu.VMEM((SB, W), bf16)],
        compiler_params=params(),
        cost_estimate=cost(2 * rows * W * WP, 36 * MiB),
        name="first_backward",
    )(crop, a, db, p, v, x)


def input_grad_kernel(da_ref, f_ref, dv_ref, out_ref):
    total = dv_ref[...]
    for j in range(NB):
        total = total + nn(
            da_ref[:, j * SP : j * SP + SB], f_ref[j * SB : (j + 1) * SB, :]
        )
    out_ref[...] = total


def input_gradient(da, f, dv):
    rows = da.shape[0]
    return pl.pallas_call(
        input_grad_kernel,
        grid=(pl.cdiv(W, SP),),
        in_specs=[
            pl.BlockSpec((rows, WP), lambda j: (0, 0)),
            pl.BlockSpec((W, SP), lambda j: (0, j)),
            pl.BlockSpec((rows, SP), lambda j: (0, j)),
        ],
        out_specs=pl.BlockSpec((rows, SP), lambda j: (0, j)),
        out_shape=jax.ShapeDtypeStruct((rows, W), f32),
        compiler_params=params(),
        cost_estimate=cost(2 * rows * W * WP, 32 * MiB),
        name="input_gradient",
    )(da, f, dv)


def place_rows(crop, parity, own):
    row = lax.broadcasted_iota(jnp.int32, (HALF, 2 * OWN), 0)
    at = lax.broadcasted_iota(jnp.int32, (HALF, 2 * OWN), 1)
    core = crop if own else 1 - crop
    return (at == 2 * (row + HALF * core) + parity).astype(f32).astype(bf16)


def adam_kernel(crop_ref, scale_ref, *refs):
    own, other, (p_ref, m_ref, v_ref), outs = refs[:4], refs[4:8], refs[8:11], refs[11:14]
    crop = crop_ref[0]
    step = pl.program_id(0)
    g_scr = refs[14]
    place = {(o, h): place_rows(crop, h, o) for o in (True, False) for h in (0, 1)}

    def turned(k, cols, parity):
        return tn(own[k][:, cols], place[True, parity]) + tn(
            other[k][:, cols], place[False, parity]
        )

    @pl.when(step == 0)
    def _():
        g_scr[...] = turned(0, slice(0, W // 2), 0)
        g_scr[...] += turned(0, slice(896, W), 1)[W // 2 - 896 :]

    @pl.when(step == 1)
    def _():
        for j in range(NB):
            cols = slice(j * SP, (j + 1) * SP)
            for parity in (0, 1):
                low = max(j * SB, parity * (W // 2))
                high = min((j + 1) * SB, (parity + 1) * (W // 2))
                if low < high:
                    part = turned(1, cols, parity)[low - j * SB : high - j * SB]
                    at = low - parity * (W // 2)
                    if parity == 0:
                        g_scr[at : at + high - low, :] = part
                    else:
                        g_scr[at : at + high - low, :] += part

    @pl.when(step == 2)
    def _():
        half = R // 2
        for n, (k, first) in enumerate(((2, 0), (3, 0), (3, RP))):
            cols = slice(first, first + RP)
            g_scr[n * half : (n + 1) * half, :] = (
                turned(k, cols, 0)[:half] + turned(k, cols, 1)[half : 2 * half]
            )

    gradient = scale_ref[0] * g_scr[...]
    first_new = beta_one * m_ref[...] + (1.0 - beta_one) * gradient
    second_new = beta_two * v_ref[...] + (1.0 - beta_two) * gradient * gradient
    corrected = (
        first_new
        / (1.0 - beta_one**STEP)
        / (jnp.sqrt(second_new / (1.0 - beta_two**STEP)) + adam_epsilon)
    )
    parameter = p_ref[...]
    outs[0][...] = parameter - rate_matrix * (corrected + decay_matrix * parameter)
    outs[1][...] = first_new
    outs[2][...] = second_new


def adam_packed(crop, factor, own, other, packed, first, second):
    columns, rows = packed.shape
    block = pl.BlockSpec((W // 2, rows), lambda i: (i, 0))
    whole = pl.BlockSpec(memory_space=pltpu.VMEM)
    shape = jax.ShapeDtypeStruct((columns, rows), f32)
    return pl.pallas_call(
        adam_kernel,
        grid=(pl.cdiv(columns, W // 2),),
        in_specs=[SCALAR, SCALAR] + [whole] * 8 + [block] * 3,
        out_specs=[block] * 3,
        out_shape=[shape] * 3,
        scratch_shapes=[pltpu.VMEM((W // 2, rows), f32)],
        compiler_params=params(),
        cost_estimate=cost(30 * columns * rows, 20 * MiB),
        name="adam_packed",
    )(crop, factor, *own, *other, packed, first, second)


def exchanges(value, combine):
    value = combine(value, lax.ppermute(value, "crop", [(0, 1), (1, 0)]))
    count = lax.axis_size("pix")
    step = 1
    while step < count:
        pairs = [(i, i ^ step) for i in range(count)]
        value = combine(value, lax.ppermute(value, "pix", pairs))
        step *= 2
    return value


def add_all(value):
    return exchanges(value, lambda a, b: a + b)


def join_moments(a, b):
    n = a[2] + b[2]
    gap = b[0] - a[0]
    mean = (a[2] * a[0] + b[2] * b[0]) / n
    squares = (a[1] + b[1]) + gap * gap * (a[2] * b[2] / n)
    return jnp.stack([mean, squares, n])


def moments_all(stats, count):
    full = jnp.concatenate([stats, jnp.full((1, stats.shape[1]), count)], axis=0)
    full = exchanges(full, join_moments)
    inverse = lax.rsqrt(full[1] / full[2] + epsilon_norm)
    return full[0], inverse, full[2, 0]


def pad_channels(vec):
    lead = vec.shape[:-1]
    blocks = vec.reshape(lead + (NB, SB))
    return jnp.pad(blocks, [(0, 0)] * len(lead) + [(0, 0), (0, SP - SB)]).reshape(lead + (WP,))


def cut_channels(vec):
    lead = vec.shape[:-1]
    return vec.reshape(lead + (NB, SP))[..., :SB].reshape(lead + (W,))


def rows_of(*vectors):
    block = jnp.stack(vectors)
    return jnp.pad(block, ((0, 8 - len(vectors)), (0, 0)))


def pad_last(block):
    rows = block.shape[0]
    return jnp.pad(block.reshape(rows, NB, SB), ((0, 0), (0, 0), (0, SP - SB))).reshape(rows, WP)


def cut_last(block):
    rows = block.shape[0]
    return block.reshape(rows, NB, SP)[:, :, :SB].reshape(rows, W)


def split_packed(packed):
    half = W // 2
    kernel_end = W + 9 * GW // 2
    edges = (0, half, W, kernel_end, kernel_end + R // 2, packed.shape[1])
    return [packed[:, a:b] for a, b in zip(edges[:-1], edges[1:])]


def pad_units(squeeze, excite):
    wide = ((0, 0), (0, RP - R))
    return jnp.concatenate([jnp.pad(squeeze, wide), jnp.pad(excite, wide)], axis=1)


def aligned(rows):
    return rows % 4 == 0


def bit_of(step):
    return (lax.axis_index("pix") // step) % 2


def across(value, step):
    pairs = [(i, i ^ step) for i in range(lax.axis_size("pix"))]
    return lax.ppermute(value, "pix", pairs)


def other_core(value):
    return lax.ppermute(value, "crop", [(0, 1), (1, 0)])


def all_steps():
    count = lax.axis_size("pix")
    return [1 << i for i in reversed(range(count.bit_length() - 1))]


def gather_pairs(block, order):
    have = []
    held = block
    for step in order:
        got = across(held, step)
        have = sorted(have + [step], reverse=True)
        upper = bit_of(step) == 1
        held = jnp.stack(
            [jnp.where(upper, got, held), jnp.where(upper, held, got)], axis=have.index(step)
        )
    return held.reshape((lax.axis_size("pix"),) + block.shape)


def reduce_pairs(keep, send, order):
    left = all_steps()
    lead = (2,) * len(left)
    ours = keep.reshape(lead + keep.shape[1:])
    theirs = other_core(send).reshape(ours.shape)

    def added(bit, axis):
        one, two = (
            lax.dynamic_index_in_dim(part, bit, axis, keepdims=False) for part in (ours, theirs)
        )
        return (one.astype(f32) + two.astype(f32)).astype(bf16)

    for step in order:
        axis = left.index(step)
        left.remove(step)
        bit = bit_of(step)
        got = across(added(1 - bit, axis), step)
        ours, theirs = added(bit, axis), got
    return (ours.astype(f32) + theirs.astype(f32)).astype(bf16)


def order_of(text):
    steps = {"x": 1, "y": 2, "4": 4, "8": 8}
    return [steps[c] for c in text]


def owned_rows(matrix):
    blocks = matrix.reshape(OWNERS, OWN, matrix.shape[1])
    return jnp.pad(blocks, ((0, 0), (0, 2 * HALF - OWN), (0, 0)))


def whole_rows(blocks):
    return blocks[:, :OWN].reshape(W, blocks.shape[2])


def gather_weights(packed):
    rows = packed.shape[0]
    blocks = split_packed(packed.astype(bf16))
    if rows != 2 * OWN:
        whole = [lax.all_gather(b, "pix", axis=0, tiled=True) for b in blocks]
        first, third, kernel, squeeze, excite = (b.reshape(W, -1) for b in whole)
        kernel = jnp.pad(kernel, ((0, 0), (0, KP - 9 * GW)))
        return (
            owned_rows(first), owned_rows(pad_last(third)), kernel, pad_units(squeeze, excite)
        )
    mine = lax.axis_index("crop")

    def own_half(block):
        block = jnp.pad(block, ((0, 2 * HALF - OWN), (0, 0)))
        return lax.dynamic_slice_in_dim(block, mine * HALF, HALF, 0)

    def gather(block):
        got = lax.all_gather(own_half(block), ("pix", "crop"), axis=0, tiled=True)
        return got.reshape(OWNERS, 2 * HALF, block.shape[1])

    def gather_by_pairs(block, order):
        held = gather_pairs(own_half(block), order)
        got = other_core(held)
        both = jnp.stack(
            [jnp.where(mine == 1, got, held), jnp.where(mine == 1, held, got)], axis=1
        )
        return whole_rows(both.reshape(OWNERS, 2 * HALF, block.shape[1]))

    first, third, kernel, squeeze, excite = (b.reshape(OWN, -1) for b in blocks)
    first = gather(first)
    kernel = gather_by_pairs(jnp.pad(kernel, ((0, 0), (0, KP - 9 * GW))), order_of("8yx4"))
    wide = ((0, 0), (0, RP - R))
    squeeze = gather_by_pairs(jnp.pad(squeeze, wide), order_of("48yx"))
    excite = gather_by_pairs(jnp.pad(excite, wide), order_of("8x4y"))
    third = gather(pad_last(third))
    return first, third, kernel, jnp.concatenate([squeeze, excite], axis=1)


def adam_step(parameter, gradient, first_moment, second_moment, step_rate, decay_rate):
    first_new = beta_one * first_moment + (1.0 - beta_one) * gradient
    second_new = beta_two * second_moment + (1.0 - beta_two) * gradient * gradient
    corrected = (
        first_new
        / (1.0 - beta_one**STEP)
        / (jnp.sqrt(second_new / (1.0 - beta_two**STEP)) + adam_epsilon)
    )
    return (parameter - step_rate * (corrected + decay_rate * parameter), first_new, second_new)


def update_packed(gf, gl, gk, gqe, packed, moment_one, moment_two, vector_squares):
    crop = lax.axis_index("crop")
    rows = packed.shape[0]
    if rows != 2 * OWN:

        def joined(pairs):
            both = [
                jnp.stack([jnp.where(crop == 0, k, s), jnp.where(crop == 0, s, k)], axis=1)
                for k, s in pairs
            ]
            wide = jnp.concatenate(both, axis=-1)
            return whole_rows(wide.reshape(OWNERS, 2 * HALF, wide.shape[-1]))

        gf, gk, gqe = (joined(g) for g in (gf, gk, gqe))
        gl = cut_last(whole_rows(gl.reshape(OWNERS, 2 * HALF, WP)))
        parts = (gf, gl, gk[:, : 9 * GW], gqe[:, :R], gqe[:, RP : RP + R])
        packed_grad = jnp.concatenate([g.reshape(2 * W, -1) for g in parts], axis=1)
        owned = lax.psum_scatter(packed_grad, "pix", scatter_dimension=0, tiled=True)
        owned = lax.psum(owned, "crop").astype(f32)
        grad_norm = jnp.sqrt(lax.psum(jnp.sum(owned * owned), "pix") + vector_squares)
        factor = jnp.minimum(1.0, clip_bound / (grad_norm + 1e-06))
        new = adam_step(packed, factor * owned, moment_one, moment_two, rate_matrix, decay_matrix)
        return new, grad_norm, factor

    third = lax.psum_scatter(
        gl.reshape(2 * OWNERS, HALF, WP), ("pix", "crop"), scatter_dimension=0, tiled=False
    )
    units = [reduce_pairs(*pair, order_of(o)) for pair, o in zip(gqe, ("4xy8", "y4x8"))]
    kernel = reduce_pairs(*gk[0], order_of("xy84"))
    first = [reduce_pairs(*pair, order_of(o)) for pair, o in zip(gf, ("4xy8", "y4x8", "xy84"))]
    own = [jnp.concatenate(first, axis=1), third, kernel, jnp.concatenate(units, axis=1)]
    squared = sum(jnp.sum(jnp.square(h.astype(f32))) for h in own)
    other = [other_core(h) for h in own]
    squared = add_all(jnp.full((8, 128), squared))[0, 0]
    grad_norm = jnp.sqrt(squared + vector_squares)
    factor = jnp.minimum(1.0, clip_bound / (grad_norm + 1e-06))
    new = adam_packed(
        crop.reshape(1), factor.reshape(1), own, other, packed.T, moment_one.T, moment_two.T
    )
    return tuple(a.T for a in new), grad_norm, factor


def local(
    inputs,
    out_grad,
    pixel_mask,
    crop_source,
    packed,
    moment_one,
    moment_two,
    vector,
    vector_one,
    vector_two,
):
    images = inputs.shape[1]
    rows = images * PIX
    total_images = images * lax.axis_size("pix")
    x = inputs.reshape(rows, W)
    og = out_grad.reshape(rows, W)
    mask = pixel_mask.reshape(images, PIX).astype(f32)
    v = jnp.broadcast_to(mask.reshape(rows, 1), (rows, 128))
    ninv = 1.0 / jnp.sum(mask, axis=1)[:, None]
    local_count = jnp.sum(mask)
    crop = lax.axis_index("crop")
    pix = lax.axis_index("pix")

    gains = vector[: 3 * W].reshape(3, W)
    shifts = vector[3 * W : 6 * W].reshape(3, W)
    gains_wide = pad_channels(gains)
    shifts_wide = pad_channels(shifts)
    eb = pad_channels(vector[6 * W : 7 * W]).reshape(NB, 1, SP)
    qb = jnp.pad(vector[7 * W :], (0, RP - R))[None, :]

    first, third, kernel, units = gather_weights(packed)
    sources = gather_pairs(crop_source, all_steps()).reshape(-1)
    every = jnp.arange(total_images, dtype=jnp.int32)
    counts = jnp.sum((sources[:, None] == every[None, :]).astype(f32), axis=0)
    mine = pix * images + jnp.arange(images, dtype=jnp.int32)
    hits = jnp.where(
        crop == 1, crop_source[:, None] == every[None, :], mine[:, None] == sources[None, :]
    ).astype(bf16)
    wanted = jnp.where(crop == 1, crop_source, mine)
    divisor = jnp.sum((wanted[:, None] == every[None, :]).astype(f32) * counts[None, :], axis=1)
    align = (align_weight / jnp.maximum(divisor, 1.0))[:, None]

    a1, stats, first = first_matmul(x, first, v)
    mean1, inv1, n = moments_all(stats, local_count)
    fwd1 = rows_of(mean1, inv1 * gains_wide[0], shifts_wide[0])
    c, stats = conv_forward(a1, fwd1, v, kernel)
    mean2, inv2, _ = moments_all(stats, local_count)
    fwd2 = rows_of(mean2, inv2 * gains_wide[1], shifts_wide[1])
    a3, stats, sp, zp, z, gate, third = third_matmul(c, fwd2, v, ninv, units, eb, qb, third)
    mean3, inv3, _ = moments_all(stats, local_count)
    fwd3 = rows_of(mean3, inv3, gains[2], shifts[2])
    output, per_image, og_sums = output_pass(a3, x, og, fwd3, v, ninv)
    per_image = per_image.transpose(1, 0, 2, 3).reshape(3, images, W)

    other = other_core(per_image[0].astype(bf16))
    half = W // 256 * 128 + 128
    orders = (order_of("x8y4"), order_of("8x4y")) if images * 16 == total_images else [all_steps()] * 2
    parts = [
        nn(hits, gather_pairs(block, order).reshape(total_images, -1))
        for block, order in zip((other[:, :half], other[:, half:]), orders)
    ]
    den = jnp.concatenate(parts, axis=1) * align * ninv

    sums3 = add_all(
        og_sums
        + jnp.stack([jnp.sum(den * per_image[2], axis=0), jnp.sum(den * per_image[1], axis=0)])
    )
    back3 = rows_of(
        mean3, inv3, gains[2], shifts[2], gains[2] * inv3, sums3[1] / n, sums3[0] / n
    )
    fwd2 = rows_of(mean2, inv2, gains_wide[1], shifts_wide[1])
    dv, gl, du, im = third_backward(a3, x, og, back3, v, den, third, c, fwd2, gate)
    which = crop.reshape(1)
    pgn, sums2, gqb, *gqe = excite_backward(which, im, gate, zp, z, sp, units, ninv)
    sums2 = sums2.transpose(1, 0, 2).reshape(3, WP)
    sums2 = add_all(jnp.concatenate([sums2, jnp.pad(gqb, ((0, 0), (0, WP - RP)))], axis=0))
    back2 = rows_of(
        mean2, inv2, gains_wide[1], shifts_wide[1], gains_wide[1] * inv2, sums2[1] / n,
        sums2[0] / n,
    )
    fwd1 = rows_of(mean1, inv1, gains_wide[0], shifts_wide[0])
    db1, sums1, *gk = conv_backward(which, a1, c, du, fwd1, back2, v, gate, pgn, kernel)
    sums1 = add_all(sums1)
    back1 = rows_of(
        mean1, inv1, gains_wide[0], shifts_wide[0], gains_wide[0] * inv1, sums1[1] / n,
        sums1[0] / n,
    )
    da1, *gf = first_backward(which, a1, db1, back1, v, x)
    input_grad = input_gradient(da1, first, dv)

    vector_grad = jnp.concatenate(
        [
            cut_channels(sums1[0]),
            cut_channels(sums2[0]),
            sums3[0],
            cut_channels(sums1[1]),
            cut_channels(sums2[1]),
            sums3[1],
            cut_channels(sums2[2]),
            sums2[3, :R],
        ]
    )
    gf, gk, gqe = (list(zip(g[: len(g) // 2], g[len(g) // 2 :])) for g in (gf, gk, gqe))
    (packed_new, moment_one_new, moment_two_new), grad_norm, factor = update_packed(
        gf, gl, gk, gqe, packed, moment_one, moment_two, jnp.sum(vector_grad * vector_grad)
    )
    vector_new, vector_first, vector_second = adam_step(
        vector, factor * vector_grad, vector_one, vector_two, rate_vector, 0.0
    )
    return (
        output.reshape(inputs.shape),
        input_grad.reshape(inputs.shape),
        packed_new,
        moment_one_new,
        moment_two_new,
        vector_new,
        vector_first,
        vector_second,
        grad_norm,
    )


def solution(mesh):
    in_specs = (
        P("crop", "pix", None, None),
        P("crop", "pix", None, None),
        P("crop", "pix", None),
        P("pix"),
        P("pix", None),
        P("pix", None),
        P("pix", None),
        P(),
        P(),
        P(),
    )
    out_specs = (
        P("crop", "pix", None, None),
        P("crop", "pix", None, None),
        P("pix", None),
        P("pix", None),
        P("pix", None),
        P(),
        P(),
        P(),
        P(),
    )
    return jax.shard_map(local, mesh=mesh, in_specs=in_specs, out_specs=out_specs, check_vma=False)
```
